32 devices in a mesh: dom: 4 (over y, x), tile: 8 (over z, core).
Axes of the slice: x: 2, y: 2, z: 4, core: 2. Of those that a mesh axis runs over, the one named last changes fastest.
Arguments:
- atm_anom: bfloat16 [128, 80, 127, 128], P(('dom', 'tile')), may hold values from -0.25 to 0.25
- ocn_anom: bfloat16 [128, 80, 75, 128], P(('dom', 'tile')), may hold values from -0.25 to 0.25
- atm_vec: bfloat16 [128, 127, 128], P(('dom', 'tile')), may hold values from -6 to 6
- ocn_vec: bfloat16 [128, 75, 128], P(('dom', 'tile')), may hold values from -6 to 6
- atm_to_ocean: int32 [128, 128], P(('dom', 'tile')), may hold values from 0 to 16383, as said below
- sea_tiles: int32 [128], P(('dom', 'tile')), may hold values 0 or 1
- atm_class: int32 [128, 5], P(('dom', 'tile')), may hold values from 0 to 4
- ocn_class: int32 [128, 5], P(('dom', 'tile')), may hold values from 0 to 4
Outputs:
- atm_out: float32 [128, 127, 128], P(('dom', 'tile'))
- ocn_out: float32 [128, 75, 128], P(('dom', 'tile'))
The draws below stay inside these ranges and needn't reach their ends.
Inputs may be any that keep to these rules, and one draw needn't show every extreme that they name: atm_to_ocean is one to one onto all 16384 ocean columns; the atmosphere columns held by the r-th device along dom+tile (tiles r * 4 to r * 4 + 3) are paired exactly with the ocean columns whose column index c satisfies c // (128 / number of devices) = r.
All inputs are finite; a program needn't handle non-finite values. No bound on the sum of `sea_tiles` on one device may be relied on, other than what follows from the above.
Results may differ from the reference program's by a relative error of at most 0.0029.
Values may be sent and summed in bfloat16 or wider, within the bound.
No kernel may reach another device: no remote copies, remote signals or barrier semaphores. Data moves between devices by JAX's collectives and lax.ppermute only.
A program may use at most 64 MiB of HBM per device.

```python
import jax
import jax.numpy as jnp
from jax import lax

M = 80
LA = 127
LO = 75
C = 128
KA = 16
KO = 16
HALO = 2
TILE_DEV = 4
TILES = 128
N_DOM = 4
N_TILE = 8


def draw_atm_to_ocean(key, part):
    device_count = N_DOM * N_TILE
    per_peer = C // device_count
    slot_count = TILE_DEV * C

    def one_sender(sender):
        shuffled = jax.random.permutation(jax.random.fold_in(key, sender), slot_count).astype(jnp.int32)
        dest_local = shuffled // C
        position = shuffled % C
        dest_device = position // per_peer
        column = sender * per_peer + position % per_peer
        return ((dest_device * TILE_DEV + dest_local) * C + column).astype(jnp.int32)
    paired = jax.vmap(one_sender)(jnp.arange(device_count, dtype=jnp.int32))
    return paired.reshape(TILES, C)


def with_ends(drawn, own_key, smallest, high):
    dims = drawn.shape
    spot = [jax.random.randint(jax.random.fold_in(own_key, axis), (), 0, dims[axis]) for axis in range(len(dims))]
    drawn = drawn.at[tuple(spot)].set(smallest)
    longest = dims.index(max(dims))
    spot[longest] = (spot[longest] + 1) % dims[longest]
    return drawn.at[tuple(spot)].set(high)


def shard_levels(own_key, dims, pieces, least, high):
    factor_of = 1.0
    for axis_at, parts in pieces:
        draws = jax.random.uniform(jax.random.fold_in(jax.random.fold_in(own_key, 6), axis_at), (parts,), jnp.float32, least / len(pieces), high / len(pieces))
        factor_of = factor_of * jnp.repeat(jnp.exp(draws), dims[axis_at] // parts).reshape((-1,) + (1,) * (len(dims) - 1 - axis_at))
    return factor_of


def scatter_about(own_key, dims, scale, reach, pieces=(), kind=jnp.bfloat16):
    entries = jax.random.normal(own_key, dims, jnp.float32) * scale
    if len(pieces) > 0:
        entries = shard_levels(own_key, dims, pieces, -0.22, 0.18) * entries
    return jnp.clip(entries, min=-reach, max=reach).astype(kind)


def setup_inputs(seed: int = 0) -> dict:
    seeds = jax.random.split(jax.random.key(seed), 9)
    atm_anom = scatter_about(seeds[0], (TILES, M, LA, C), 0.04, 0.25, ((0, 32),))
    ocn_anom = scatter_about(seeds[1], (TILES, M, LO, C), 0.04, 0.25, ((0, 32),))
    atm_vec = scatter_about(seeds[2], (TILES, LA, C), 1.0, 6.0, ((0, 32),))
    ocn_vec = scatter_about(seeds[3], (TILES, LO, C), 1.0, 6.0, ((0, 32),))
    atm_to_ocean = draw_atm_to_ocean(jax.random.fold_in(seeds[8], 71), 0)
    sea_tiles = with_ends((jax.random.randint(seeds[5], (TILES,), 0, 4) < 3).astype(jnp.int32), jax.random.fold_in(seeds[5], 1), 0, 1)
    atm_class = with_ends(jax.random.randint(seeds[6], (TILES, 2 * HALO + 1), 0, 5), jax.random.fold_in(seeds[6], 1), 0, 4).astype(jnp.int32)
    ocn_class = with_ends(jax.random.randint(seeds[7], (TILES, 2 * HALO + 1), 0, 5), jax.random.fold_in(seeds[7], 1), 0, 4).astype(jnp.int32)
    return dict(atm_anom=atm_anom, ocn_anom=ocn_anom, atm_vec=atm_vec, ocn_vec=ocn_vec, atm_to_ocean=atm_to_ocean, sea_tiles=sea_tiles, atm_class=atm_class, ocn_class=ocn_class)


COUPLING = 8.0
ATM_SPREAD = 12.0
OCN_SPREAD = 8.0
CLASS_TABLE = (1.0, 0.7, 0.45, 0.25, 0.0)


def level_taper(level_count, spread):
    position = jnp.arange(level_count, dtype=jnp.float32)
    scaled = (position[:, None] - position[None, :]) / spread
    return jnp.exp(-0.5 * scaled * scaled)


def class_weights(classes):
    class_table = jnp.array(CLASS_TABLE, jnp.float32)
    matches = classes[..., None] == jnp.arange(len(CLASS_TABLE), dtype=jnp.int32)
    return jnp.sum(jnp.where(matches, class_table, 0.0), axis=-1)


def horizontal(coefficients, classes):
    weights = class_weights(classes)
    band_view = coefficients.reshape((N_DOM, N_TILE * TILE_DEV) + coefficients.shape[1:])
    summed = jnp.zeros_like(coefficients)
    for offset in range(-HALO, HALO + 1):
        rolled = jnp.roll(band_view, -offset, axis=1).reshape(coefficients.shape)
        summed = summed + weights[:, offset + HALO, None, None] * rolled
    return summed


def intra_apply(anomaly, vector, classes, tapering):
    coefficients = lax.map(lambda tile_pair: jnp.einsum("mlc,lc->ml", tile_pair[0].astype(jnp.float32), tile_pair[1].astype(jnp.float32)), (anomaly, vector))
    spread = horizontal(coefficients, classes)
    vertical_coeff = jnp.einsum("tmk,lk->tml", spread, tapering, precision=lax.Precision.HIGHEST).astype(jnp.bfloat16)
    return lax.map(lambda tile_pair: jnp.einsum("mlc,ml->lc", tile_pair[0].astype(jnp.float32), tile_pair[1].astype(jnp.float32)), (anomaly, vertical_coeff))


def reference(atm_anom, ocn_anom, atm_vec, ocn_vec, atm_to_ocean, sea_tiles, atm_class, ocn_class):
    ocean = ocn_anom * sea_tiles.astype(jnp.bfloat16)[:, None, None, None]
    atm_inc = intra_apply(atm_anom, atm_vec, atm_class, level_taper(LA, ATM_SPREAD))
    ocn_inc = intra_apply(ocean, ocn_vec, ocn_class, level_taper(LO, OCN_SPREAD))
    rise_position = jnp.arange(KA, dtype=jnp.float32)
    rise_weights = jnp.exp(-2.0 * (KA - 1 - rise_position) / KA)
    fall_position = jnp.arange(KO, dtype=jnp.float32)
    fall_weights = jnp.exp(-2.0 * fall_position / KO)
    atm_surface = atm_anom[:, :, LA - KA:, :].astype(jnp.float32)
    ocn_top = ocean[:, :, :KO, :].astype(jnp.float32)
    atm_weighted = atm_vec[:, LA - KA:, :].astype(jnp.float32) * rise_weights[None, :, None]
    ocn_weighted = ocn_vec[:, :KO, :].astype(jnp.float32) * fall_weights[None, :, None]
    atm_proj = jnp.einsum("tmsc,tsc->mtc", atm_surface, atm_weighted).astype(jnp.bfloat16)
    ocn_proj = jnp.einsum("tmoc,toc->mtc", ocn_top, ocn_weighted).astype(jnp.bfloat16)
    flat_width = TILES * C
    pairing = atm_to_ocean.reshape(flat_width).astype(jnp.int32)
    ocean_pair = jnp.zeros((M, flat_width), jnp.bfloat16).at[:, pairing].set(atm_proj.reshape(M, flat_width)).reshape(M, TILES, C)
    atm_pair = ocn_proj.reshape(M, flat_width)[:, pairing].reshape(M, TILES, C)
    atm_cross = COUPLING * rise_weights[None, :, None] * jnp.einsum("tmsc,mtc->tsc", atm_surface, atm_pair.astype(jnp.float32))
    ocn_cross = COUPLING * fall_weights[None, :, None] * jnp.einsum("tmoc,mtc->toc", ocn_top, ocean_pair.astype(jnp.float32))
    atm_out = atm_inc.at[:, LA - KA:, :].add(atm_cross)
    ocn_out = ocn_inc.at[:, :KO, :].add(ocn_cross)
    return (atm_out, ocn_out)
```

```python
import functools
import math

import jax
import jax.numpy as jnp
from jax import lax
from jax.experimental import pallas as pl
from jax.experimental.pallas import tpu as pltpu
from jax.sharding import PartitionSpec as P

KA = 16
KO = 16
HALO = 2

COUPLING = 8.0
ATM_SPREAD = 12.0
OCN_SPREAD = 8.0
CLASS_TABLE = (1.0, 0.7, 0.45, 0.25, 0.0)

BF16 = jnp.bfloat16
F32 = jnp.float32
MIB = 1 << 20
NT = (((1,), (1,)), ((), ()))
TN = (((0,), (0,)), ((), ()))
VMEM_SPEC = pl.BlockSpec(memory_space=pltpu.VMEM)
SMEM_SPEC = pl.BlockSpec(memory_space=pltpu.SMEM)
ANY_SPEC = pl.BlockSpec(memory_space=pl.ANY)

RISE = [math.exp(-2.0 * (KA - 1 - s) / KA) for s in range(KA)]
FALL = [math.exp(-2.0 * o / KO) for o in range(KO)]


def slot_rows(index, columns, tiles, per_peer):
    tile, column = index // columns, index % columns
    return (tile // tiles) * (tiles * per_peer) + (tile % tiles) * per_peer + column % per_peer


def one_hot(rows, width):
    position = lax.broadcasted_iota(jnp.int32, (width, rows.shape[1]), 0)
    return jnp.where(position == rows, 1.0, 0.0).astype(BF16)


def atm_slots(pairing_ref, columns, tiles, per_peer):
    index = jnp.concatenate([pairing_ref[t : t + 1, :] for t in range(tiles)], axis=1)
    return one_hot(slot_rows(index, columns, tiles, per_peer), tiles * columns)


def ocn_slots(columns, tiles, per_peer):
    place = lax.broadcasted_iota(jnp.int32, (1, tiles * columns), 1)
    tile, column = place // columns, place % columns
    rows = (column // per_peer) * (tiles * per_peer) + tile * per_peer + column % per_peer
    return one_hot(rows, tiles * columns)


def first_kernel(
    per_peer,
    sea_ref,
    pairing_ref,
    atm_vec_ref,
    ocn_vec_ref,
    atm_hbm,
    ocn_hbm,
    atm_ref,
    ocn_ref,
    low_ref,
    high_ref,
    atm_send_ref,
    ocn_send_ref,
    vec_ref,
    weight_ref,
    sems,
):
    tiles, atm_levels, members, columns = atm_hbm.shape
    ocn_levels = ocn_hbm.shape[1]
    copies = {}
    for t in range(tiles):
        copies["a", t] = pltpu.make_async_copy(atm_hbm.at[t], atm_ref.at[t], sems.at[0, t])
        copies["o", t] = pltpu.make_async_copy(ocn_hbm.at[t], ocn_ref.at[t], sems.at[1, t])
    for t in range(tiles):
        copies["a", t].start()
    for t in range(tiles):
        copies["o", t].start()

    lane = lax.broadcasted_iota(jnp.int32, (members, columns), 1)
    weight_ref[...] = jnp.zeros_like(weight_ref)

    def load_vec(source_ref, t, levels):
        vec_ref[...] = jnp.zeros_like(vec_ref)
        vec_ref[:levels] = source_ref[:, t, :].astype(F32)

    def coefficients(ref, t, levels):
        half = (levels + 1) // 2
        second = levels - half
        vec_t = vec_ref[...].T.astype(BF16)
        weight_ref[:columns, :columns] = vec_t
        weight_ref[columns:, columns:] = vec_t
        rows = jnp.concatenate(
            [
                ref[t, 0:half].reshape(half * members, columns),
                ref[t, second:levels].reshape(half * members, columns),
            ],
            axis=1,
        )
        product = jnp.dot(rows, weight_ref[...], preferred_element_type=F32)
        total = jnp.zeros((members, columns), F32)
        for j in range(half):
            part = product[j * members : (j + 1) * members]
            total = jnp.where(lane == j, part[:, :columns], total)
            total = jnp.where(lane == second + j, part[:, columns:], total)
        return total

    def projection(ref, t, start, weights):
        total = jnp.zeros((members, columns), F32)
        for s, weight in enumerate(weights):
            row = vec_ref[start + s : start + s + 1, :] * weight
            total = total + ref[t, start + s].astype(F32) * row
        return total

    def store(t, which, value):
        if t < tiles // 2:
            high_ref[t, which] = value
        else:
            low_ref[t - tiles // 2, which] = value

    atm_proj = []
    for t in range(tiles):
        load_vec(atm_vec_ref, t, atm_levels)
        copies["a", t].wait()
        store(t, 0, coefficients(atm_ref, t, atm_levels))
        atm_proj.append(projection(atm_ref, t, atm_levels - KA, RISE).astype(BF16))
    atm_send_ref[...] = lax.dot_general(
        atm_slots(pairing_ref, columns, tiles, per_peer),
        jnp.concatenate(atm_proj, axis=1),
        NT,
        preferred_element_type=F32,
    ).astype(BF16)
    ocn_proj = []
    for t in range(tiles):
        load_vec(ocn_vec_ref, t, ocn_levels)
        sea = sea_ref[t].astype(F32)
        copies["o", t].wait()
        store(t, 1, coefficients(ocn_ref, t, ocn_levels) * sea)
        ocn_proj.append((projection(ocn_ref, t, 0, FALL) * sea).astype(BF16))
    ocn_send_ref[...] = lax.dot_general(
        ocn_slots(columns, tiles, per_peer),
        jnp.concatenate(ocn_proj, axis=1),
        NT,
        preferred_element_type=F32,
    ).astype(BF16)


def second_kernel(
    sea_ref,
    atm_class_ref,
    ocn_class_ref,
    atm_ref,
    ocn_ref,
    low_ref,
    own_low_ref,
    own_high_ref,
    high_ref,
    atm_out_ref,
    ocn_out_ref,
    vert_ref,
):
    tiles, atm_levels, members, columns = atm_ref.shape
    ocn_levels = ocn_ref.shape[1]
    padded = [(low_ref, 0), (low_ref, 1), (own_low_ref, 0), (own_low_ref, 1)]
    padded += [(own_high_ref, 0), (own_high_ref, 1), (high_ref, 0), (high_ref, 1)]
    group = 16
    sub = lax.broadcasted_iota(jnp.int32, (group, columns), 0)
    row = lax.broadcasted_iota(jnp.int32, (columns, columns), 0)
    col = lax.broadcasted_iota(jnp.int32, (columns, columns), 1)

    def class_weight(number):
        weight = jnp.float32(0.0)
        for value, factor in enumerate(CLASS_TABLE):
            weight = jnp.where(number == value, jnp.float32(factor), weight)
        return weight

    def taper(spread):
        scaled = (row - col).astype(F32) * (1.0 / spread)
        return jnp.exp(-0.5 * scaled * scaled)

    for which, (ref, out_ref, class_ref, levels, width) in enumerate(
        [
            (atm_ref, atm_out_ref, atm_class_ref, atm_levels, ATM_SPREAD),
            (ocn_ref, ocn_out_ref, ocn_class_ref, ocn_levels, OCN_SPREAD),
        ]
    ):
        tapering = taper(width)
        for t in range(tiles):
            spread = jnp.zeros((members, columns), F32)
            for offset in range(2 * HALO + 1):
                source, place = padded[t + offset]
                spread = spread + class_weight(class_ref[t, offset]) * source[place, which]
            vert_ref[t] = lax.dot_general(
                tapering, spread, NT, precision=lax.Precision.HIGHEST, preferred_element_type=F32
            ).astype(BF16)

        @pl.loop(0, tiles)
        def _(t):
            sea = sea_ref[t].astype(F32)
            for start in range(0, levels, group):
                count = min(group, levels - start)
                right = jnp.concatenate([ref[t, start + j] for j in range(count)], axis=1)
                product = jnp.dot(
                    vert_ref[t, start : start + group, :], right, preferred_element_type=F32
                )
                total = product[:, :columns]
                for j in range(1, count):
                    total = jnp.where(sub == j, product[:, j * columns : (j + 1) * columns], total)
                if which == 1:
                    total = total * sea
                out_ref[start : start + count, t, :] = total[:count]


def cross_kernel(
    per_peer,
    sea_ref,
    pairing_ref,
    atm_recv_ref,
    ocn_recv_ref,
    atm_top_hbm,
    ocn_top_hbm,
    atm_in,
    ocn_in,
    atm_out,
    ocn_out,
    atm_top,
    ocn_top,
    atm_rows,
    ocn_rows,
    sems,
):
    tiles, atm_levels, members, columns = atm_top_hbm.shape
    start = atm_levels - KA
    loads = [
        pltpu.make_async_copy(atm_in.at[pl.ds(start, KA)], atm_rows, sems.at[0]),
        pltpu.make_async_copy(ocn_in.at[pl.ds(0, KO)], ocn_rows, sems.at[1]),
        pltpu.make_async_copy(atm_top_hbm.at[:, pl.ds(start, KA)], atm_top, sems.at[2]),
        pltpu.make_async_copy(ocn_top_hbm.at[:, pl.ds(0, KO)], ocn_top, sems.at[3]),
    ]
    for load in loads:
        load.start()
    atm_pair = lax.dot_general(
        ocn_recv_ref[...],
        atm_slots(pairing_ref, columns, tiles, per_peer),
        TN,
        preferred_element_type=F32,
    )
    ocn_pair = lax.dot_general(
        atm_recv_ref[...],
        ocn_slots(columns, tiles, per_peer),
        TN,
        preferred_element_type=F32,
    )
    for load in loads:
        load.wait()

    def add(top, rows, pair, weights, scale):
        for t in range(tiles):
            paired = pair[:, t * columns : (t + 1) * columns]
            sums = [
                jnp.sum(top[t, s].astype(F32) * paired, axis=0, keepdims=True) * (COUPLING * weight)
                for s, weight in enumerate(weights)
            ]
            rows[:, t, :] = rows[:, t, :] + jnp.concatenate(sums, axis=0) * scale(t)

    add(atm_top, atm_rows, atm_pair, RISE, lambda t: jnp.float32(1.0))
    add(ocn_top, ocn_rows, ocn_pair, FALL, lambda t: sea_ref[t].astype(F32))
    stores = [
        pltpu.make_async_copy(atm_rows, atm_out.at[pl.ds(start, KA)], sems.at[0]),
        pltpu.make_async_copy(ocn_rows, ocn_out.at[pl.ds(0, KO)], sems.at[1]),
    ]
    for store in stores:
        store.start()
    for store in stores:
        store.wait()


def local(atm_anom, ocn_anom, atm_vec, ocn_vec, atm_to_ocean, sea_tiles, atm_class, ocn_class):
    tiles, members, atm_levels, columns = atm_anom.shape
    ocn_levels = ocn_anom.shape[2]
    axes = ("dom", "tile")
    devices = lax.axis_size("dom") * lax.axis_size("tile")
    per_peer = columns // devices
    peer_rows = tiles * per_peer
    slots = tiles * columns

    by_level = (0, 2, 1, 3)
    atm = jnp.transpose(atm_anom, by_level)
    ocn = jnp.transpose(ocn_anom, by_level)
    atm_rows = jnp.transpose(atm_vec, (1, 0, 2))
    ocn_rows = jnp.transpose(ocn_vec, (1, 0, 2))

    edge = jax.ShapeDtypeStruct((tiles // 2, 2, members, columns), F32)
    send = jax.ShapeDtypeStruct((slots, members), BF16)
    atm_v, ocn_v, own_high, own_low, atm_send, ocn_send = pl.pallas_call(
        functools.partial(first_kernel, per_peer),
        out_shape=[
            pltpu.VMEM(atm.shape, BF16),
            pltpu.VMEM(ocn.shape, BF16),
            edge,
            edge,
            send,
            send,
        ],
        in_specs=[SMEM_SPEC, VMEM_SPEC, VMEM_SPEC, VMEM_SPEC, ANY_SPEC, ANY_SPEC],
        out_specs=[VMEM_SPEC] * 6,
        scratch_shapes=[
            pltpu.VMEM((columns, columns), F32),
            pltpu.VMEM((2 * columns, 2 * columns), BF16),
            pltpu.SemaphoreType.DMA((2, tiles)),
        ],
        compiler_params=pltpu.CompilerParams(vmem_limit_bytes=44 * MIB),
        name="first_pass",
    )(sea_tiles, atm_to_ocean, atm_rows, ocn_rows, atm, ocn)

    count = lax.axis_size("tile")
    forward = [(i, (i + 1) % count) for i in range(count)]
    backward = [(target, source) for source, target in forward]
    low = lax.ppermute(own_high, "tile", forward)
    high = lax.ppermute(own_low, "tile", backward)

    outgoing = jnp.concatenate(
        [
            atm_send.reshape(devices, peer_rows, members),
            ocn_send.reshape(devices, peer_rows, members),
        ],
        axis=1,
    )
    incoming = lax.all_to_all(outgoing, axes, split_axis=0, concat_axis=0, tiled=True)
    atm_recv = incoming[:, :peer_rows].reshape(slots, members)
    ocn_recv = incoming[:, peer_rows:].reshape(slots, members)

    elements = tiles * members * columns * (atm_levels + ocn_levels)
    outs = [
        jax.ShapeDtypeStruct((atm_levels, tiles, columns), F32),
        jax.ShapeDtypeStruct((ocn_levels, tiles, columns), F32),
    ]
    atm_out, ocn_out = pl.pallas_call(
        second_kernel,
        out_shape=outs,
        in_specs=[SMEM_SPEC] * 3 + [VMEM_SPEC] * 6,
        out_specs=[VMEM_SPEC] * 2,
        scratch_shapes=[pltpu.VMEM((tiles, columns, members), BF16)],
        compiler_params=pltpu.CompilerParams(vmem_limit_bytes=24 * MIB),
        cost_estimate=pl.CostEstimate(
            flops=2 * 16 * elements, bytes_accessed=2 * elements, transcendentals=0
        ),
        name="second_pass",
    )(sea_tiles, atm_class, ocn_class, atm_v, ocn_v, low, own_low, own_high, high)

    atm_out, ocn_out = pl.pallas_call(
        functools.partial(cross_kernel, per_peer),
        out_shape=outs,
        in_specs=[SMEM_SPEC] + [VMEM_SPEC] * 3 + [ANY_SPEC] * 4,
        out_specs=[ANY_SPEC] * 2,
        input_output_aliases={6: 0, 7: 1},
        scratch_shapes=[
            pltpu.VMEM((tiles, KA, members, columns), BF16),
            pltpu.VMEM((tiles, KO, members, columns), BF16),
            pltpu.VMEM((KA, tiles, columns), F32),
            pltpu.VMEM((KO, tiles, columns), F32),
            pltpu.SemaphoreType.DMA((4,)),
        ],
        compiler_params=pltpu.CompilerParams(vmem_limit_bytes=24 * MIB),
        name="surface_cross",
    )(sea_tiles, atm_to_ocean, atm_recv, ocn_recv, atm, ocn, atm_out, ocn_out)
    return jnp.transpose(atm_out, (1, 0, 2)), jnp.transpose(ocn_out, (1, 0, 2))


def solution(mesh):
    in_specs = (
        P(("dom", "tile"), None, None, None),
        P(("dom", "tile"), None, None, None),
        P(("dom", "tile"), None, None),
        P(("dom", "tile"), None, None),
        P(("dom", "tile"), None),
        P(("dom", "tile")),
        P(("dom", "tile"), None),
        P(("dom", "tile"), None),
    )
    out_specs = (P(("dom", "tile"), None, None), P(("dom", "tile"), None, None))
    return jax.shard_map(local, mesh=mesh, in_specs=in_specs, out_specs=out_specs, check_vma=False)
```

```python
import functools
import math

import jax
import jax.numpy as jnp
from jax import lax
from jax.experimental import pallas as pl
from jax.experimental.pallas import tpu as pltpu
from jax.sharding import PartitionSpec as P

KA = 16
KO = 16
HALO = 2
GROUP = 8

COUPLING = 8.0
ATM_SPREAD = 12.0
OCN_SPREAD = 8.0
CLASS_TABLE = (1.0, 0.7, 0.45, 0.25, 0.0)

BF16 = jnp.bfloat16
F32 = jnp.float32
MIB = 1 << 20
NT = (((1,), (1,)), ((), ()))
TN = (((0,), (0,)), ((), ()))
VMEM_SPEC = pl.BlockSpec(memory_space=pltpu.VMEM)
SMEM_SPEC = pl.BlockSpec(memory_space=pltpu.SMEM)
ANY_SPEC = pl.BlockSpec(memory_space=pl.ANY)

RISE = [math.exp(-2.0 * (KA - 1 - s) / KA) for s in range(KA)]
FALL = [math.exp(-2.0 * o / KO) for o in range(KO)]


def slot_rows(index, columns, tiles, per_peer):
    tile, column = index // columns, index % columns
    return (tile // tiles) * (tiles * per_peer) + (tile % tiles) * per_peer + column % per_peer


def one_hot(rows, width):
    position = lax.broadcasted_iota(jnp.int32, (width, rows.shape[1]), 0)
    return jnp.where(position == rows, 1.0, 0.0).astype(BF16)


def atm_slots(pairing_ref, columns, tiles, per_peer):
    index = jnp.concatenate([pairing_ref[t : t + 1, :] for t in range(tiles)], axis=1)
    return one_hot(slot_rows(index, columns, tiles, per_peer), tiles * columns)


def ocn_slots(columns, tiles, per_peer):
    place = lax.broadcasted_iota(jnp.int32, (1, tiles * columns), 1)
    tile, column = place // columns, place % columns
    rows = (column // per_peer) * (tiles * per_peer) + tile * per_peer + column % per_peer
    return one_hot(rows, tiles * columns)


def in_vmem(array):
    return pltpu.with_memory_space_constraint(array, pltpu.VMEM)


def tile_copies(source, target, sems):
    return [
        pltpu.make_async_copy(source.at[t], target.at[t], sems.at[t]) for t in range(source.shape[0])
    ]


def spread_vectors(source, vec_ref, which, tiles):
    levels, _, columns = source.shape
    for t in range(tiles):
        place = which * tiles + t
        vec_ref[place, :levels] = source[:, t, :].astype(F32)
        if levels < columns:
            vec_ref[place, levels:] = jnp.zeros((columns - levels, columns), F32)


def project_kernel(
    per_peer,
    sea_hbm,
    pairing_hbm,
    atm_vec_hbm,
    ocn_vec_hbm,
    atm_hbm,
    ocn_hbm,
    send_ref,
    atm_top,
    ocn_top,
    sems,
    sea_ref,
    pairing_ref,
    atm_vec_ref,
    ocn_vec_ref,
    small_sems,
):
    tiles, atm_levels, members, columns = atm_hbm.shape
    start = atm_levels - KA
    peers, count = send_ref.shape[0], send_ref.shape[1] // 2
    small = [
        pltpu.make_async_copy(pairing_hbm, pairing_ref, small_sems.at[0]),
        pltpu.make_async_copy(atm_vec_hbm.at[pl.ds(start, KA)], atm_vec_ref, small_sems.at[1]),
        pltpu.make_async_copy(ocn_vec_hbm.at[pl.ds(0, KO)], ocn_vec_ref, small_sems.at[2]),
        pltpu.make_async_copy(sea_hbm, sea_ref, small_sems.at[3]),
    ]
    for load in small:
        load.start()
    loads = [
        [
            pltpu.make_async_copy(atm_hbm.at[t, pl.ds(start, KA)], atm_top.at[t], sems.at[0, t]),
            pltpu.make_async_copy(ocn_hbm.at[t, pl.ds(0, KO)], ocn_top.at[t], sems.at[1, t]),
        ]
        for t in range(tiles)
    ]
    for pair in loads:
        for load in pair:
            load.start()
    for load in small:
        load.wait()
    slots = [
        atm_slots(pairing_ref, columns, tiles, per_peer),
        ocn_slots(columns, tiles, per_peer),
    ]
    atm_rows = atm_vec_ref[...].astype(F32)
    ocn_rows = ocn_vec_ref[...].astype(F32)

    def projection(top, t, rows, weights):
        total = jnp.zeros((members, columns), F32)
        for s, weight in enumerate(weights):
            total = total + top[t, s].astype(F32) * (rows[s, t : t + 1, :] * weight)
        return total

    atm_proj, ocn_proj = [], []
    for t in range(tiles):
        for load in loads[t]:
            load.wait()
        atm_proj.append(projection(atm_top, t, atm_rows, RISE).astype(BF16))
        sea = sea_ref[t].astype(F32)
        ocn_proj.append((projection(ocn_top, t, ocn_rows, FALL) * sea).astype(BF16))
    for place, proj in enumerate([atm_proj, ocn_proj]):
        rows = lax.dot_general(
            slots[place], jnp.concatenate(proj, axis=1), NT, preferred_element_type=F32
        ).astype(BF16)
        send_ref[:, place * count : (place + 1) * count, :] = rows.reshape(peers, count, members)


def first_kernel(
    sea_hbm,
    atm_vec_hbm,
    ocn_vec_hbm,
    atm_hbm,
    ocn_hbm,
    inner_ref,
    outer_ref,
    atm_ref,
    ocn_ref,
    sea_ref,
    atm_vec_ref,
    ocn_vec_ref,
    vec_ref,
    weight_ref,
    small_sems,
    atm_sems,
    ocn_sems,
):
    tiles, atm_levels, members, columns = atm_hbm.shape
    ocn_levels = ocn_hbm.shape[1]
    small = [
        pltpu.make_async_copy(atm_vec_hbm, atm_vec_ref, small_sems.at[0]),
        pltpu.make_async_copy(ocn_vec_hbm, ocn_vec_ref, small_sems.at[1]),
        pltpu.make_async_copy(sea_hbm, sea_ref, small_sems.at[2]),
    ]
    for load in small:
        load.start()
    atm_copies = tile_copies(atm_hbm, atm_ref, atm_sems)
    ocn_copies = tile_copies(ocn_hbm, ocn_ref, ocn_sems)
    for copy in atm_copies + ocn_copies:
        copy.start()
    even = lax.rem(lax.axis_index("tile"), 2) == 0
    lane = lax.broadcasted_iota(jnp.int32, (members, columns), 1)

    zeros = jnp.zeros((columns, columns), BF16)
    for load in small:
        load.wait()
    spread_vectors(atm_vec_ref, vec_ref, 0, tiles)
    spread_vectors(ocn_vec_ref, vec_ref, 1, tiles)
    for place in range(2 * tiles):
        vec_t = vec_ref[place].T.astype(BF16)
        weight_ref[place, :columns, :columns] = vec_t
        weight_ref[place, :columns, columns:] = zeros
        weight_ref[place, columns:, :columns] = zeros
        weight_ref[place, columns:, columns:] = vec_t

    def coefficients(ref, t, place, levels):
        half = (levels + 1) // 2
        second = levels - half
        total = jnp.zeros((members, columns), F32)
        for first in range(0, half, GROUP):
            count = min(GROUP, half - first)
            left = ref[t, first : first + count].reshape(count * members, columns)
            right = ref[t, second + first : second + first + count].reshape(count * members, columns)
            product = jnp.dot(
                jnp.concatenate([left, right], axis=1),
                weight_ref[place],
                preferred_element_type=F32,
            )
            for j in range(count):
                part = product[j * members : (j + 1) * members]
                total = jnp.where(lane == first + j, part[:, :columns], total)
                total = jnp.where(lane == second + first + j, part[:, columns:], total)
        return total

    def store(t, which, value):
        lower = t < tiles // 2
        slot = t if lower else t - tiles // 2

        @pl.when(jnp.logical_not(even) if lower else even)
        def _():
            inner_ref[slot, which] = value

        @pl.when(even if lower else jnp.logical_not(even))
        def _():
            outer_ref[slot, which] = value

    for t in range(tiles):
        atm_copies[t].wait()
        store(t, 0, coefficients(atm_ref, t, t, atm_levels))
    for t in range(tiles):
        ocn_copies[t].wait()
        sea = sea_ref[t].astype(F32)
        store(t, 1, coefficients(ocn_ref, t, tiles + t, ocn_levels) * sea)


def second_kernel(
    sea_ref,
    atm_class_ref,
    ocn_class_ref,
    inner_ref,
    outer_ref,
    inner_recv_ref,
    outer_recv_ref,
    atm_cross_ref,
    ocn_cross_ref,
    atm_hbm,
    ocn_hbm,
    atm_out_hbm,
    ocn_out_hbm,
    atm_ref,
    ocn_ref,
    atm_out_ref,
    ocn_out_ref,
    padded_ref,
    vert_ref,
    out_sems,
    atm_sems,
    ocn_sems,
):
    tiles, atm_levels, members, columns = atm_hbm.shape
    ocn_levels = ocn_hbm.shape[1]
    atm_copies = tile_copies(atm_hbm, atm_ref, atm_sems)
    ocn_copies = tile_copies(ocn_hbm, ocn_ref, ocn_sems)
    for copy in atm_copies + ocn_copies:
        copy.start()
    even = lax.rem(lax.axis_index("tile"), 2) == 0
    quarter = tiles // 2

    @pl.when(even)
    def _():
        for place, ref in enumerate([outer_recv_ref, outer_ref, inner_ref, inner_recv_ref]):
            padded_ref[place * quarter : (place + 1) * quarter] = ref[...]

    @pl.when(jnp.logical_not(even))
    def _():
        for place, ref in enumerate([inner_recv_ref, inner_ref, outer_ref, outer_recv_ref]):
            padded_ref[place * quarter : (place + 1) * quarter] = ref[...]

    group = 16
    sub = lax.broadcasted_iota(jnp.int32, (group, columns), 0)
    row = lax.broadcasted_iota(jnp.int32, (columns, columns), 0)
    col = lax.broadcasted_iota(jnp.int32, (columns, columns), 1)

    def class_weight(number):
        weight = jnp.float32(0.0)
        for value, factor in enumerate(CLASS_TABLE):
            weight = jnp.where(number == value, jnp.float32(factor), weight)
        return weight

    def taper(spread):
        scaled = (row - col).astype(F32) * (1.0 / spread)
        return jnp.exp(-0.5 * scaled * scaled)

    stores = [
        pltpu.make_async_copy(atm_out_ref, atm_out_hbm, out_sems.at[0]),
        pltpu.make_async_copy(ocn_out_ref, ocn_out_hbm, out_sems.at[1]),
    ]
    parts = [
        (atm_ref, atm_copies, atm_out_ref, atm_class_ref, atm_levels, ATM_SPREAD),
        (ocn_ref, ocn_copies, ocn_out_ref, ocn_class_ref, ocn_levels, OCN_SPREAD),
    ]
    for which, (_, _, _, class_ref, _, width) in enumerate(parts):
        tapering = taper(width)
        for t in range(tiles):
            spread = jnp.zeros((members, columns), F32)
            for offset in range(2 * HALO + 1):
                spread = spread + class_weight(class_ref[t, offset]) * padded_ref[t + offset, which]
            vert_ref[which, t] = lax.dot_general(
                tapering, spread, NT, precision=lax.Precision.HIGHEST, preferred_element_type=F32
            ).astype(BF16)

    for which, (ref, copies, out_ref, _, levels, _) in enumerate(parts):
        for t in range(tiles):
            copies[t].wait()
            for start in range(0, levels, group):
                count = min(group, levels - start)
                right = jnp.concatenate([ref[t, start + j] for j in range(count)], axis=1)
                product = jnp.dot(
                    vert_ref[which, t, start : start + group, :], right, preferred_element_type=F32
                )
                total = product[:, :columns]
                for j in range(1, count):
                    total = jnp.where(sub == j, product[:, j * columns : (j + 1) * columns], total)
                if which == 1:
                    total = total * sea_ref[t].astype(F32)
                out_ref[start : start + count, t, :] = total[:count]
        if which == 0:
            surface = levels - KA
            out_ref[surface:] = out_ref[surface:] + atm_cross_ref[...]
        else:
            out_ref[:KO] = out_ref[:KO] + ocn_cross_ref[...]
        stores[which].start()
    for store in stores:
        store.wait()


def cross_kernel(
    per_peer,
    sea_ref,
    pairing_ref,
    recv_ref,
    atm_hbm,
    ocn_hbm,
    atm_cross_ref,
    ocn_cross_ref,
    atm_top,
    ocn_top,
    sems,
):
    tiles, atm_levels, members, columns = atm_hbm.shape
    start = atm_levels - KA
    loads = [
        [
            pltpu.make_async_copy(atm_hbm.at[t, pl.ds(start, KA)], atm_top.at[t], sems.at[0, t]),
            pltpu.make_async_copy(ocn_hbm.at[t, pl.ds(0, KO)], ocn_top.at[t], sems.at[1, t]),
        ]
        for t in range(tiles)
    ]
    for pair in loads:
        for load in pair:
            load.start()
    peers, count = recv_ref.shape[0], recv_ref.shape[1] // 2

    def pair_columns(first, slots):
        rows = recv_ref[:, first : first + count, :].reshape(peers * count, members)
        return lax.dot_general(rows, slots, TN, preferred_element_type=F32)

    atm_pair = pair_columns(count, atm_slots(pairing_ref, columns, tiles, per_peer))
    ocn_pair = pair_columns(0, ocn_slots(columns, tiles, per_peer))

    def rows_of(top, t, paired, weights):
        part = paired[:, t * columns : (t + 1) * columns]
        sums = [
            jnp.sum(top[t, s].astype(F32) * part, axis=0, keepdims=True) * (COUPLING * weight)
            for s, weight in enumerate(weights)
        ]
        return jnp.concatenate(sums, axis=0)

    for t in range(tiles):
        for load in loads[t]:
            load.wait()
        atm_cross_ref[:, t, :] = rows_of(atm_top, t, atm_pair, RISE)
        ocn_cross_ref[:, t, :] = rows_of(ocn_top, t, ocn_pair, FALL) * sea_ref[t].astype(F32)


def local(atm_anom, ocn_anom, atm_vec, ocn_vec, atm_to_ocean, sea_tiles, atm_class, ocn_class):
    tiles, members, atm_levels, columns = atm_anom.shape
    ocn_levels = ocn_anom.shape[2]
    axes = ("dom", "tile")
    devices = lax.axis_size("dom") * lax.axis_size("tile")
    per_peer = columns // devices
    peer_rows = tiles * per_peer

    by_level = (0, 2, 1, 3)
    atm = jnp.transpose(atm_anom, by_level)
    ocn = jnp.transpose(ocn_anom, by_level)
    atm_rows = jnp.transpose(atm_vec, (1, 0, 2))
    ocn_rows = jnp.transpose(ocn_vec, (1, 0, 2))
    params = pltpu.CompilerParams(vmem_limit_bytes=58 * MIB)

    elements = tiles * members * columns * (atm_levels + ocn_levels)
    top_elements = tiles * members * columns * (KA + KO)
    tops = [
        pltpu.VMEM((tiles, KA, members, columns), BF16),
        pltpu.VMEM((tiles, KO, members, columns), BF16),
        pltpu.SemaphoreType.DMA((2, tiles)),
    ]
    wholes = [pltpu.VMEM(atm.shape, BF16), pltpu.VMEM(ocn.shape, BF16)]
    whole_sems = [pltpu.SemaphoreType.DMA((tiles,)), pltpu.SemaphoreType.DMA((tiles,))]

    def cost(flops, count):
        return pl.CostEstimate(flops=flops, bytes_accessed=2 * count, transcendentals=0)

    outgoing = pl.pallas_call(
        functools.partial(project_kernel, per_peer),
        out_shape=pltpu.VMEM((devices, 2 * peer_rows, members), BF16),
        in_specs=[ANY_SPEC] * 6,
        out_specs=VMEM_SPEC,
        scratch_shapes=tops
        + [
            pltpu.SMEM(sea_tiles.shape, jnp.int32),
            pltpu.VMEM(atm_to_ocean.shape, jnp.int32),
            pltpu.VMEM((KA, tiles, columns), BF16),
            pltpu.VMEM((KO, tiles, columns), BF16),
            pltpu.SemaphoreType.DMA((4,)),
        ],
        compiler_params=params,
        cost_estimate=cost(4 * top_elements, top_elements),
        name="project",
    )(sea_tiles, atm_to_ocean, atm_rows, ocn_rows, atm, ocn)
    incoming = lax.all_to_all(outgoing, axes, split_axis=0, concat_axis=0, tiled=True)

    edge = pltpu.VMEM((tiles // 2, 2, members, columns), F32)
    inner, outer = pl.pallas_call(
        first_kernel,
        out_shape=[edge, edge],
        in_specs=[ANY_SPEC] * 5,
        out_specs=[VMEM_SPEC] * 2,
        scratch_shapes=wholes
        + [
            pltpu.SMEM(sea_tiles.shape, jnp.int32),
            pltpu.VMEM(atm_rows.shape, BF16),
            pltpu.VMEM(ocn_rows.shape, BF16),
            pltpu.VMEM((2 * tiles, columns, columns), F32),
            pltpu.VMEM((2 * tiles, 2 * columns, 2 * columns), BF16),
            pltpu.SemaphoreType.DMA((3,)),
        ]
        + whole_sems,
        compiler_params=params,
        cost_estimate=cost(2 * 256 * elements, elements),
        name="first_pass",
    )(sea_tiles, atm_rows, ocn_rows, atm, ocn)

    count = lax.axis_size("tile")
    outer_pairs = [(i, (i + 1) % count if i % 2 else (i - 1) % count) for i in range(count)]
    outer_recv = lax.ppermute(outer, "tile", outer_pairs)
    inner_recv = lax.ppermute(inner, "tile", [(i, i ^ 1) for i in range(count)])

    atm_cross, ocn_cross = pl.pallas_call(
        functools.partial(cross_kernel, per_peer),
        out_shape=[
            pltpu.VMEM((KA, tiles, columns), F32),
            pltpu.VMEM((KO, tiles, columns), F32),
        ],
        in_specs=[SMEM_SPEC, VMEM_SPEC, VMEM_SPEC] + [ANY_SPEC] * 2,
        out_specs=[VMEM_SPEC] * 2,
        scratch_shapes=tops,
        compiler_params=params,
        cost_estimate=cost(40 * top_elements, 4 * top_elements),
        name="surface_cross",
    )(sea_tiles, atm_to_ocean, in_vmem(incoming), atm, ocn)

    atm_out, ocn_out = pl.pallas_call(
        second_kernel,
        out_shape=[
            jax.ShapeDtypeStruct((atm_levels, tiles, columns), F32),
            jax.ShapeDtypeStruct((ocn_levels, tiles, columns), F32),
        ],
        in_specs=[SMEM_SPEC] * 3 + [VMEM_SPEC] * 6 + [ANY_SPEC] * 2,
        out_specs=[ANY_SPEC] * 2,
        scratch_shapes=wholes
        + [
            pltpu.VMEM((atm_levels, tiles, columns), F32),
            pltpu.VMEM((ocn_levels, tiles, columns), F32),
            pltpu.VMEM((2 * tiles, 2, members, columns), F32),
            pltpu.VMEM((2, tiles, columns, members), BF16),
            pltpu.SemaphoreType.DMA((2,)),
        ]
        + whole_sems,
        compiler_params=params,
        cost_estimate=cost(2 * 256 * elements, elements),
        name="second_pass",
    )(
        sea_tiles,
        atm_class,
        ocn_class,
        in_vmem(inner),
        in_vmem(outer),
        in_vmem(inner_recv),
        in_vmem(outer_recv),
        in_vmem(atm_cross),
        in_vmem(ocn_cross),
        atm,
        ocn,
    )
    return jnp.transpose(atm_out, (1, 0, 2)), jnp.transpose(ocn_out, (1, 0, 2))


def solution(mesh):
    in_specs = (
        P(("dom", "tile"), None, None, None),
        P(("dom", "tile"), None, None, None),
        P(("dom", "tile"), None, None),
        P(("dom", "tile"), None, None),
        P(("dom", "tile"), None),
        P(("dom", "tile")),
        P(("dom", "tile"), None),
        P(("dom", "tile"), None),
    )
    out_specs = (P(("dom", "tile"), None, None), P(("dom", "tile"), None, None))
    return jax.shard_map(local, mesh=mesh, in_specs=in_specs, out_specs=out_specs, check_vma=False)
```

```python
import functools
import math

import jax
import jax.numpy as jnp
from jax import lax
from jax.experimental import pallas as pl
from jax.experimental.pallas import tpu as pltpu
from jax.sharding import PartitionSpec as P

KA = 16
KO = 16
HALO = 2
GROUP = 8
ATM_REGIONS = [[0], [1], [2], [3]]
REGIONS = [[(0, 0)], [(0, 1), (0, 2)], [(0, 3), (1, 0)], [(1, 1), (1, 2), (1, 3)]]

COUPLING = 8.0
ATM_SPREAD = 12.0
OCN_SPREAD = 8.0
CLASS_TABLE = (1.0, 0.7, 0.45, 0.25, 0.0)

BF16 = jnp.bfloat16
F32 = jnp.float32
MIB = 1 << 20
NT = (((1,), (1,)), ((), ()))
TN = (((0,), (0,)), ((), ()))
VMEM_SPEC = pl.BlockSpec(memory_space=pltpu.VMEM)
SMEM_SPEC = pl.BlockSpec(memory_space=pltpu.SMEM)
ANY_SPEC = pl.BlockSpec(memory_space=pl.ANY)

RISE = [math.exp(-2.0 * (KA - 1 - s) / KA) for s in range(KA)]
FALL = [math.exp(-2.0 * o / KO) for o in range(KO)]


def slot_rows(index, columns, tiles, per_peer):
    tile, column = index // columns, index % columns
    return (tile // tiles) * (tiles * per_peer) + (tile % tiles) * per_peer + column % per_peer


def one_hot(rows, width):
    position = lax.broadcasted_iota(jnp.int32, (width, rows.shape[1]), 0)
    return jnp.where(position == rows, 1.0, 0.0).astype(BF16)


def atm_slots(pairing_ref, columns, tiles, per_peer):
    index = jnp.concatenate([pairing_ref[t : t + 1, :] for t in range(tiles)], axis=1)
    return one_hot(slot_rows(index, columns, tiles, per_peer), tiles * columns)


def ocn_slots(columns, tiles, per_peer):
    place = lax.broadcasted_iota(jnp.int32, (1, tiles * columns), 1)
    tile, column = place // columns, place % columns
    rows = (column // per_peer) * (tiles * per_peer) + tile * per_peer + column % per_peer
    return one_hot(rows, tiles * columns)


def in_vmem(array):
    return pltpu.with_memory_space_constraint(array, pltpu.VMEM)


def tile_copies(source, target, sems):
    return [
        pltpu.make_async_copy(source.at[t], target.at[t], sems.at[t]) for t in range(source.shape[0])
    ]


def spread_vectors(source, vec_ref, which, tiles):
    levels, _, columns = source.shape
    for t in range(tiles):
        place = which * tiles + t
        vec_ref[place, :levels] = source[:, t, :].astype(F32)
        if levels < columns:
            vec_ref[place, levels:] = jnp.zeros((columns - levels, columns), F32)


def project_kernel(
    per_peer,
    sea_hbm,
    pairing_hbm,
    atm_vec_hbm,
    ocn_vec_hbm,
    atm_hbm,
    ocn_hbm,
    send_ref,
    atm_top,
    ocn_top,
    sems,
    sea_ref,
    pairing_ref,
    atm_vec_ref,
    ocn_vec_ref,
    small_sems,
):
    tiles, atm_levels, members, columns = atm_hbm.shape
    start = atm_levels - KA
    peers, count = send_ref.shape[0], send_ref.shape[1] // 2
    small = [
        pltpu.make_async_copy(pairing_hbm, pairing_ref, small_sems.at[0]),
        pltpu.make_async_copy(atm_vec_hbm.at[pl.ds(start, KA)], atm_vec_ref, small_sems.at[1]),
        pltpu.make_async_copy(ocn_vec_hbm.at[pl.ds(0, KO)], ocn_vec_ref, small_sems.at[2]),
        pltpu.make_async_copy(sea_hbm, sea_ref, small_sems.at[3]),
    ]
    for load in small:
        load.start()
    loads = [
        [
            pltpu.make_async_copy(atm_hbm.at[t, pl.ds(start, KA)], atm_top.at[t], sems.at[0, t]),
            pltpu.make_async_copy(ocn_hbm.at[t, pl.ds(0, KO)], ocn_top.at[t], sems.at[1, t]),
        ]
        for t in range(tiles)
    ]
    for pair in loads:
        for load in pair:
            load.start()
    for load in small:
        load.wait()
    slots = [
        atm_slots(pairing_ref, columns, tiles, per_peer),
        ocn_slots(columns, tiles, per_peer),
    ]
    atm_rows = atm_vec_ref[...].astype(F32)
    ocn_rows = ocn_vec_ref[...].astype(F32)

    def projection(top, t, rows, weights):
        total = jnp.zeros((members, columns), F32)
        for s, weight in enumerate(weights):
            total = total + top[t, s].astype(F32) * (rows[s, t : t + 1, :] * weight)
        return total

    atm_proj, ocn_proj = [], []
    for t in range(tiles):
        for load in loads[t]:
            load.wait()
        atm_proj.append(projection(atm_top, t, atm_rows, RISE).astype(BF16))
        sea = sea_ref[t].astype(F32)
        ocn_proj.append((projection(ocn_top, t, ocn_rows, FALL) * sea).astype(BF16))
    for place, proj in enumerate([atm_proj, ocn_proj]):
        rows = lax.dot_general(
            slots[place], jnp.concatenate(proj, axis=1), NT, preferred_element_type=F32
        ).astype(BF16)
        send_ref[:, place * count : (place + 1) * count, :] = rows.reshape(peers, count, members)


def first_kernel(
    sea_hbm,
    atm_vec_hbm,
    ocn_vec_hbm,
    atm_hbm,
    ocn_hbm,
    inner_ref,
    outer_ref,
    atm_ref,
    ocn_ref,
    sea_ref,
    atm_vec_ref,
    ocn_vec_ref,
    vec_ref,
    weight_ref,
    coeff_ref,
    small_sems,
    atm_sems,
    ocn_sems,
):
    tiles, atm_levels, members, columns = atm_hbm.shape
    ocn_levels = ocn_hbm.shape[1]
    small = [
        pltpu.make_async_copy(atm_vec_hbm, atm_vec_ref, small_sems.at[0]),
        pltpu.make_async_copy(ocn_vec_hbm, ocn_vec_ref, small_sems.at[1]),
        pltpu.make_async_copy(sea_hbm, sea_ref, small_sems.at[2]),
    ]
    for load in small:
        load.start()
    atm_copies = tile_copies(atm_hbm, atm_ref, atm_sems)
    ocn_copies = tile_copies(ocn_hbm, ocn_ref, ocn_sems)
    copies = [atm_copies, ocn_copies]
    for region in REGIONS[:2]:
        for which, t in region:
            copies[which][t].start()
    even = lax.rem(lax.axis_index("tile"), 2) == 0
    lane = lax.broadcasted_iota(jnp.int32, (members, columns), 1)

    zeros = jnp.zeros((columns, columns), BF16)
    for load in small:
        load.wait()
    spread_vectors(atm_vec_ref, vec_ref, 0, tiles)
    spread_vectors(ocn_vec_ref, vec_ref, 1, tiles)
    for place in range(2 * tiles):
        vec_t = vec_ref[place].T.astype(BF16)
        weight_ref[place, :columns, :columns] = vec_t
        weight_ref[place, :columns, columns:] = zeros
        weight_ref[place, columns:, :columns] = zeros
        weight_ref[place, columns:, columns:] = vec_t

    def coefficients(ref, t, place, levels):
        half = (levels + 1) // 2
        second = levels - half
        total = jnp.zeros((members, columns), F32)
        for first in range(0, half, GROUP):
            count = min(GROUP, half - first)
            left = ref[t, first : first + count].reshape(count * members, columns)
            right = ref[t, second + first : second + first + count].reshape(count * members, columns)
            product = jnp.dot(
                jnp.concatenate([left, right], axis=1),
                weight_ref[place],
                preferred_element_type=F32,
            )
            for j in range(count):
                part = product[j * members : (j + 1) * members]
                total = jnp.where(lane == first + j, part[:, :columns], total)
                total = jnp.where(lane == second + first + j, part[:, columns:], total)
        return total

    parts = [
        (atm_ref, atm_copies, atm_levels),
        (ocn_ref, ocn_copies, ocn_levels),
    ]
    for number, region in enumerate(REGIONS):
        for which, t in region:
            parts[which][1][t].wait()
        for later in REGIONS[number + 2 : number + 2 + 1]:
            for which, t in later:
                copies[which][t].start()
        for which, t in region:
            ref, _, levels = parts[which]
            total = coefficients(ref, t, which * tiles + t, levels)
            if which == 1:
                total = total * sea_ref[t].astype(F32)
            coeff_ref[t, which] = total
    half = tiles // 2
    low, high = coeff_ref[:half], coeff_ref[half:]
    inner_ref[...] = jnp.where(even, high, low)
    outer_ref[...] = jnp.where(even, low, high)


def second_kernel(
    sea_ref,
    atm_class_ref,
    ocn_class_ref,
    inner_ref,
    outer_ref,
    inner_recv_ref,
    outer_recv_ref,
    atm_pair_ref,
    ocn_pair_ref,
    ocn_ref,
    atm_hbm,
    atm_out_hbm,
    ocn_out_hbm,
    atm_ref,
    atm_out_ref,
    ocn_out_ref,
    padded_ref,
    vert_ref,
    out_sems,
    atm_sems,
):
    tiles, atm_levels, members, columns = atm_hbm.shape
    ocn_levels = ocn_ref.shape[1]
    atm_copies = tile_copies(atm_hbm, atm_ref, atm_sems)
    for copy in atm_copies:
        copy.start()
    even = lax.rem(lax.axis_index("tile"), 2) == 0
    quarter = tiles // 2

    @pl.when(even)
    def _():
        for place, ref in enumerate([outer_recv_ref, outer_ref, inner_ref, inner_recv_ref]):
            padded_ref[place * quarter : (place + 1) * quarter] = ref[...]

    @pl.when(jnp.logical_not(even))
    def _():
        for place, ref in enumerate([inner_recv_ref, inner_ref, outer_ref, outer_recv_ref]):
            padded_ref[place * quarter : (place + 1) * quarter] = ref[...]

    group = 16
    sub = lax.broadcasted_iota(jnp.int32, (group, columns), 0)
    row = lax.broadcasted_iota(jnp.int32, (columns, columns), 0)
    col = lax.broadcasted_iota(jnp.int32, (columns, columns), 1)

    def class_weight(number):
        weight = jnp.float32(0.0)
        for value, factor in enumerate(CLASS_TABLE):
            weight = jnp.where(number == value, jnp.float32(factor), weight)
        return weight

    def taper(spread):
        scaled = (row - col).astype(F32) * (1.0 / spread)
        return jnp.exp(-0.5 * scaled * scaled)

    stores = [
        pltpu.make_async_copy(atm_out_ref, atm_out_hbm, out_sems.at[0]),
        pltpu.make_async_copy(ocn_out_ref, ocn_out_hbm, out_sems.at[1]),
    ]
    parts = [
        (atm_ref, atm_out_ref, atm_pair_ref, atm_class_ref, atm_levels, ATM_SPREAD),
        (ocn_ref, ocn_out_ref, ocn_pair_ref, ocn_class_ref, ocn_levels, OCN_SPREAD),
    ]

    def weights(which):
        _, _, _, class_ref, _, width = parts[which]
        tapering = taper(width)
        for t in range(tiles):
            spread = jnp.zeros((members, columns), F32)
            for offset in range(2 * HALO + 1):
                spread = spread + class_weight(class_ref[t, offset]) * padded_ref[t + offset, which]
            vert_ref[which, t] = lax.dot_general(
                tapering, spread, NT, precision=lax.Precision.HIGHEST, preferred_element_type=F32
            ).astype(BF16)

    def apply(which, t):
        ref, out_ref, pair_ref, _, levels, _ = parts[which]
        surface = [(levels - KA + i, RISE[i]) for i in range(KA)] if which == 0 else list(enumerate(FALL))
        coupling = dict(surface)
        paired = pair_ref[:, t * columns : (t + 1) * columns]
        for start in range(0, levels, group):
            count = min(group, levels - start)
            right = jnp.concatenate([ref[t, start + j] for j in range(count)], axis=1)
            product = jnp.dot(
                vert_ref[which, t, start : start + group, :], right, preferred_element_type=F32
            )
            total = product[:, :columns]
            for j in range(1, count):
                total = jnp.where(sub == j, product[:, j * columns : (j + 1) * columns], total)
            for j in range(count):
                if start + j in coupling:
                    term = jnp.sum(ref[t, start + j].astype(F32) * paired, axis=0, keepdims=True)
                    term = term * (COUPLING * coupling[start + j])
                    total = total + jnp.where(sub == j, term, 0.0)
            if which == 1:
                total = total * sea_ref[t].astype(F32)
            out_ref[start : start + count, t, :] = total[:count]

    def finish(which):
        stores[which].start()

    weights(1)
    weights(0)
    for t in range(tiles):
        apply(1, t)
    finish(1)
    for region in ATM_REGIONS:
        for t in region:
            atm_copies[t].wait()
        for t in region:
            apply(0, t)
    finish(0)
    for store in stores:
        store.wait()


def pair_kernel(
    per_peer,
    pairing_ref,
    recv_ref,
    ocn_hbm,
    atm_pair_ref,
    ocn_pair_ref,
    ocn_ref,
    sems,
):
    tiles, _, members, columns = ocn_hbm.shape
    ocn_copies = tile_copies(ocn_hbm, ocn_ref, sems)
    for copy in ocn_copies:
        copy.start()
    peers, count = recv_ref.shape[0], recv_ref.shape[1] // 2

    def pair_columns(first, slots):
        rows = recv_ref[:, first : first + count, :].reshape(peers * count, members)
        return lax.dot_general(rows, slots, TN, preferred_element_type=F32)

    atm_pair_ref[...] = pair_columns(count, atm_slots(pairing_ref, columns, tiles, per_peer))
    ocn_pair_ref[...] = pair_columns(0, ocn_slots(columns, tiles, per_peer))
    for copy in ocn_copies:
        copy.wait()


def local(atm_anom, ocn_anom, atm_vec, ocn_vec, atm_to_ocean, sea_tiles, atm_class, ocn_class):
    tiles, members, atm_levels, columns = atm_anom.shape
    ocn_levels = ocn_anom.shape[2]
    axes = ("dom", "tile")
    devices = lax.axis_size("dom") * lax.axis_size("tile")
    per_peer = columns // devices
    peer_rows = tiles * per_peer

    by_level = (0, 2, 1, 3)
    atm = jnp.transpose(atm_anom, by_level)
    ocn = jnp.transpose(ocn_anom, by_level)
    atm_rows = jnp.transpose(atm_vec, (1, 0, 2))
    ocn_rows = jnp.transpose(ocn_vec, (1, 0, 2))
    params = pltpu.CompilerParams(vmem_limit_bytes=58 * MIB)

    elements = tiles * members * columns * (atm_levels + ocn_levels)
    top_elements = tiles * members * columns * (KA + KO)
    tops = [
        pltpu.VMEM((tiles, KA, members, columns), BF16),
        pltpu.VMEM((tiles, KO, members, columns), BF16),
        pltpu.SemaphoreType.DMA((2, tiles)),
    ]
    wholes = [pltpu.VMEM(atm.shape, BF16), pltpu.VMEM(ocn.shape, BF16)]
    whole_sems = [pltpu.SemaphoreType.DMA((tiles,)), pltpu.SemaphoreType.DMA((tiles,))]

    def cost(flops, count):
        return pl.CostEstimate(flops=flops, bytes_accessed=2 * count, transcendentals=0)

    outgoing = pl.pallas_call(
        functools.partial(project_kernel, per_peer),
        out_shape=pltpu.VMEM((devices, 2 * peer_rows, members), BF16),
        in_specs=[ANY_SPEC] * 6,
        out_specs=VMEM_SPEC,
        scratch_shapes=tops
        + [
            pltpu.SMEM(sea_tiles.shape, jnp.int32),
            pltpu.VMEM(atm_to_ocean.shape, jnp.int32),
            pltpu.VMEM((KA, tiles, columns), BF16),
            pltpu.VMEM((KO, tiles, columns), BF16),
            pltpu.SemaphoreType.DMA((4,)),
        ],
        compiler_params=params,
        cost_estimate=cost(4 * top_elements, top_elements),
        name="project",
    )(sea_tiles, atm_to_ocean, atm_rows, ocn_rows, atm, ocn)
    incoming = lax.all_to_all(outgoing, axes, split_axis=0, concat_axis=0, tiled=True)

    edge = pltpu.VMEM((tiles // 2, 2, members, columns), F32)
    inner, outer = pl.pallas_call(
        first_kernel,
        out_shape=[edge, edge],
        in_specs=[ANY_SPEC] * 5,
        out_specs=[VMEM_SPEC] * 2,
        scratch_shapes=wholes
        + [
            pltpu.SMEM(sea_tiles.shape, jnp.int32),
            pltpu.VMEM(atm_rows.shape, BF16),
            pltpu.VMEM(ocn_rows.shape, BF16),
            pltpu.VMEM((2 * tiles, columns, columns), F32),
            pltpu.VMEM((2 * tiles, 2 * columns, 2 * columns), BF16),
            pltpu.VMEM((tiles, 2, members, columns), F32),
            pltpu.SemaphoreType.DMA((3,)),
        ]
        + whole_sems,
        compiler_params=params,
        cost_estimate=cost(2 * 256 * elements, elements),
        name="first_pass",
    )(sea_tiles, atm_rows, ocn_rows, atm, ocn)

    count = lax.axis_size("tile")
    outer_pairs = [(i, (i + 1) % count if i % 2 else (i - 1) % count) for i in range(count)]
    outer_recv = lax.ppermute(outer, "tile", outer_pairs)
    inner_recv = lax.ppermute(inner, "tile", [(i, i ^ 1) for i in range(count)])

    pair = pltpu.VMEM((members, tiles * columns), F32)
    atm_pair, ocn_pair, ocn_v = pl.pallas_call(
        functools.partial(pair_kernel, per_peer),
        out_shape=[pair, pair, pltpu.VMEM(ocn.shape, BF16)],
        in_specs=[VMEM_SPEC, VMEM_SPEC, ANY_SPEC],
        out_specs=[VMEM_SPEC] * 3,
        scratch_shapes=[pltpu.SemaphoreType.DMA((tiles,))],
        compiler_params=pltpu.CompilerParams(vmem_limit_bytes=54 * MIB),
        cost_estimate=cost(40 * top_elements, 4 * top_elements),
        name="pair_columns",
    )(atm_to_ocean, in_vmem(incoming), ocn)

    atm_out, ocn_out = pl.pallas_call(
        second_kernel,
        out_shape=[
            jax.ShapeDtypeStruct((atm_levels, tiles, columns), F32),
            jax.ShapeDtypeStruct((ocn_levels, tiles, columns), F32),
        ],
        in_specs=[SMEM_SPEC] * 3 + [VMEM_SPEC] * 7 + [ANY_SPEC],
        out_specs=[ANY_SPEC] * 2,
        scratch_shapes=[
            pltpu.VMEM(atm.shape, BF16),
            pltpu.VMEM((atm_levels, tiles, columns), F32),
            pltpu.VMEM((ocn_levels, tiles, columns), F32),
            pltpu.VMEM((2 * tiles, 2, members, columns), F32),
            pltpu.VMEM((2, tiles, columns, members), BF16),
            pltpu.SemaphoreType.DMA((2,)),
            pltpu.SemaphoreType.DMA((tiles,)),
        ],
        compiler_params=pltpu.CompilerParams(vmem_limit_bytes=50 * MIB),
        cost_estimate=cost(2 * 256 * elements, elements),
        name="second_pass",
    )(
        sea_tiles,
        atm_class,
        ocn_class,
        in_vmem(inner),
        in_vmem(outer),
        in_vmem(inner_recv),
        in_vmem(outer_recv),
        in_vmem(atm_pair),
        in_vmem(ocn_pair),
        in_vmem(ocn_v),
        atm,
    )
    return jnp.transpose(atm_out, (1, 0, 2)), jnp.transpose(ocn_out, (1, 0, 2))


def solution(mesh):
    in_specs = (
        P(("dom", "tile"), None, None, None),
        P(("dom", "tile"), None, None, None),
        P(("dom", "tile"), None, None),
        P(("dom", "tile"), None, None),
        P(("dom", "tile"), None),
        P(("dom", "tile")),
        P(("dom", "tile"), None),
        P(("dom", "tile"), None),
    )
    out_specs = (P(("dom", "tile"), None, None), P(("dom", "tile"), None, None))
    return jax.shard_map(local, mesh=mesh, in_specs=in_specs, out_specs=out_specs, check_vma=False)
```

```python
import functools
import math

import jax
import jax.numpy as jnp
from jax import lax
from jax.experimental import pallas as pl
from jax.experimental.pallas import tpu as pltpu
from jax.sharding import PartitionSpec as P

KA = 16
KO = 16
HALO = 2
GROUP = 4
VECTOR_LEVELS = (31, 19)
REGIONS = [[(0, 0)], [(0, 1), (0, 2)], [(0, 3), (1, 0)], [(1, 1), (1, 2), (1, 3)]]

COUPLING = 8.0
ATM_SPREAD = 12.0
OCN_SPREAD = 8.0
CLASS_TABLE = (1.0, 0.7, 0.45, 0.25, 0.0)

BF16 = jnp.bfloat16
F32 = jnp.float32
MIB = 1 << 20
NT = (((1,), (1,)), ((), ()))
TN = (((0,), (0,)), ((), ()))
VMEM_SPEC = pl.BlockSpec(memory_space=pltpu.VMEM)
SMEM_SPEC = pl.BlockSpec(memory_space=pltpu.SMEM)
ANY_SPEC = pl.BlockSpec(memory_space=pl.ANY)

RISE = [math.exp(-2.0 * (KA - 1 - s) / KA) for s in range(KA)]
FALL = [math.exp(-2.0 * o / KO) for o in range(KO)]


def slot_rows(index, columns, tiles, per_peer):
    tile, column = index // columns, index % columns
    return (tile // tiles) * (tiles * per_peer) + (tile % tiles) * per_peer + column % per_peer


def one_hot(rows, width):
    position = lax.broadcasted_iota(jnp.int32, (width, rows.shape[1]), 0)
    return jnp.where(position == rows, 1.0, 0.0).astype(BF16)


def atm_slots(pairing_ref, columns, tiles, per_peer):
    index = jnp.concatenate([pairing_ref[t : t + 1, :] for t in range(tiles)], axis=1)
    return one_hot(slot_rows(index, columns, tiles, per_peer), tiles * columns)


def ocn_slots(columns, tiles, per_peer):
    place = lax.broadcasted_iota(jnp.int32, (1, tiles * columns), 1)
    tile, column = place // columns, place % columns
    rows = (column // per_peer) * (tiles * per_peer) + tile * per_peer + column % per_peer
    return one_hot(rows, tiles * columns)


def in_vmem(array):
    return pltpu.with_memory_space_constraint(array, pltpu.VMEM)


def tile_copies(source, targets, sems):
    first = source.shape[0] - len(targets)
    return [
        pltpu.make_async_copy(source.at[first + i], target, sems.at[i])
        for i, target in enumerate(targets)
    ]


def each(ref):
    return [ref.at[i] for i in range(ref.shape[0])]


def spread_vectors(source, vec_ref, which, tiles):
    levels, _, columns = source.shape
    for t in range(tiles):
        place = which * tiles + t
        vec_ref[place, :levels] = source[:, t, :].astype(F32)
        if levels < columns:
            vec_ref[place, levels:] = jnp.zeros((columns - levels, columns), F32)


def project_kernel(
    per_peer,
    sea_hbm,
    pairing_hbm,
    atm_vec_hbm,
    ocn_vec_hbm,
    atm_hbm,
    ocn_hbm,
    send_ref,
    tile_ref,
    tile_vec_ref,
    atm_top,
    ocn_top,
    sems,
    sea_ref,
    pairing_ref,
    atm_vec_ref,
    ocn_vec_ref,
    small_sems,
):
    tiles, atm_levels, members, columns = atm_hbm.shape
    start = atm_levels - KA
    peers, count = send_ref.shape[0], send_ref.shape[1] // 2
    small = [
        pltpu.make_async_copy(pairing_hbm, pairing_ref, small_sems.at[0]),
        pltpu.make_async_copy(atm_vec_hbm, atm_vec_ref, small_sems.at[1]),
        pltpu.make_async_copy(ocn_vec_hbm.at[pl.ds(0, KO)], ocn_vec_ref, small_sems.at[2]),
        pltpu.make_async_copy(sea_hbm, sea_ref, small_sems.at[3]),
    ]
    for load in small:
        load.start()
    atm_tops = [tile_ref.at[pl.ds(start, KA)]] + [atm_top.at[t] for t in range(tiles - 1)]
    loads = [
        [
            pltpu.make_async_copy(atm_hbm.at[t, pl.ds(start, KA)], atm_tops[t], sems.at[0, t]),
            pltpu.make_async_copy(ocn_hbm.at[t, pl.ds(0, KO)], ocn_top.at[t], sems.at[1, t]),
        ]
        for t in range(tiles)
    ]
    for pair in loads:
        for load in pair:
            load.start()
    rest = pltpu.make_async_copy(
        atm_hbm.at[0, pl.ds(0, start)], tile_ref.at[pl.ds(0, start)], small_sems.at[4]
    )
    rest.start()
    for load in small:
        load.wait()
    slots = [
        atm_slots(pairing_ref, columns, tiles, per_peer),
        ocn_slots(columns, tiles, per_peer),
    ]
    atm_rows = atm_vec_ref[start : start + KA].astype(F32)
    ocn_rows = ocn_vec_ref[...].astype(F32)
    tile_vec_ref[:atm_levels] = atm_vec_ref[:, 0, :].astype(F32)
    if atm_levels < columns:
        tile_vec_ref[atm_levels:] = jnp.zeros((columns - atm_levels, columns), F32)

    def projection(top, t, rows, weights):
        total = jnp.zeros((members, columns), F32)
        for s, weight in enumerate(weights):
            total = total + top[s].astype(F32) * (rows[s, t : t + 1, :] * weight)
        return total

    atm_proj, ocn_proj = [], []
    for t in range(tiles):
        for load in loads[t]:
            load.wait()
        atm_proj.append(projection(atm_tops[t], t, atm_rows, RISE).astype(BF16))
        sea = sea_ref[t].astype(F32)
        ocn_proj.append((projection(ocn_top.at[t], t, ocn_rows, FALL) * sea).astype(BF16))
    for place, proj in enumerate([atm_proj, ocn_proj]):
        rows = lax.dot_general(
            slots[place], jnp.concatenate(proj, axis=1), NT, preferred_element_type=F32
        ).astype(BF16)
        send_ref[:, place * count : (place + 1) * count, :] = rows.reshape(peers, count, members)
    rest.wait()


def first_kernel(
    sea_hbm,
    atm_vec_hbm,
    ocn_vec_hbm,
    tile_ref,
    tile_vec_ref,
    atm_hbm,
    ocn_hbm,
    inner_ref,
    outer_ref,
    atm_ref,
    ocn_ref,
    sea_ref,
    atm_vec_ref,
    ocn_vec_ref,
    vec_ref,
    weight_ref,
    coeff_ref,
    small_sems,
    atm_sems,
    ocn_sems,
):
    tiles, atm_levels, members, columns = atm_hbm.shape
    ocn_levels = ocn_hbm.shape[1]
    small = [
        pltpu.make_async_copy(atm_vec_hbm, atm_vec_ref, small_sems.at[0]),
        pltpu.make_async_copy(ocn_vec_hbm, ocn_vec_ref, small_sems.at[1]),
        pltpu.make_async_copy(sea_hbm, sea_ref, small_sems.at[2]),
    ]
    for load in small:
        load.start()
    atm_copies = tile_copies(atm_hbm, each(atm_ref), atm_sems)
    ocn_copies = tile_copies(ocn_hbm, each(ocn_ref), ocn_sems)
    copies = [[None] + atm_copies, ocn_copies]
    held = [[tile_ref] + each(atm_ref), each(ocn_ref)]
    for region in REGIONS[1:3]:
        for which, t in region:
            copies[which][t].start()
    even = lax.rem(lax.axis_index("tile"), 2) == 0
    lane = lax.broadcasted_iota(jnp.int32, (members, columns), 1)

    zeros = jnp.zeros((columns, columns), BF16)

    def transpose_vectors(place):
        vec_t = vec_ref[place].T.astype(BF16)
        weight_ref[place, :columns, :columns] = vec_t
        weight_ref[place, :columns, columns:] = zeros
        weight_ref[place, columns:, :columns] = zeros
        weight_ref[place, columns:, columns:] = vec_t

    def coefficients(ref, place, levels):
        vector_levels = VECTOR_LEVELS[place // tiles]
        levels = levels - vector_levels
        half = (levels + 1) // 2
        second = levels - half
        total = jnp.zeros((members, columns), F32)
        for first in range(0, half, GROUP):
            count = min(GROUP, half - first)
            left = ref[first : first + count].reshape(count * members, columns)
            right = ref[second + first : second + first + count].reshape(count * members, columns)
            product = jnp.dot(
                jnp.concatenate([left, right], axis=1),
                weight_ref[place],
                preferred_element_type=F32,
            )
            for j in range(count):
                part = product[j * members : (j + 1) * members]
                total = jnp.where(lane == first + j, part[:, :columns], total)
                total = jnp.where(lane == second + first + j, part[:, columns:], total)
        for level in range(levels, levels + vector_levels):
            product = ref[level].astype(F32) * vec_ref[place, level : level + 1, :]
            total = jnp.where(lane == level, jnp.sum(product, axis=1, keepdims=True), total)
        return total

    level_counts = [atm_levels, ocn_levels]
    vec_ref[0] = tile_vec_ref[...]
    transpose_vectors(0)
    for number, region in enumerate(REGIONS):
        if number == 1:
            for load in small:
                load.wait()
            spread_vectors(atm_vec_ref, vec_ref, 0, tiles)
            spread_vectors(ocn_vec_ref, vec_ref, 1, tiles)
            for place in range(1, 2 * tiles):
                transpose_vectors(place)
        for which, t in region:
            if copies[which][t] is not None:
                copies[which][t].wait()
        for later in REGIONS[max(number + 2, 3) : number + 3]:
            for which, t in later:
                copies[which][t].start()
        for which, t in region:
            total = coefficients(held[which][t], which * tiles + t, level_counts[which])
            if which == 1:
                total = total * sea_ref[t].astype(F32)
            coeff_ref[t, which] = total
    half = tiles // 2
    low, high = coeff_ref[:half], coeff_ref[half:]
    inner_ref[...] = jnp.where(even, high, low)
    outer_ref[...] = jnp.where(even, low, high)


def second_kernel(
    sea_ref,
    atm_class_ref,
    ocn_class_ref,
    inner_ref,
    outer_ref,
    inner_recv_ref,
    outer_recv_ref,
    atm_pair_ref,
    ocn_pair_ref,
    ocn_ref,
    tile_ref,
    atm_hbm,
    atm_out_hbm,
    ocn_out_hbm,
    atm_ref,
    atm_out_ref,
    ocn_out_ref,
    padded_ref,
    vert_ref,
    column_ref,
    out_sems,
    atm_sems,
):
    tiles, atm_levels, members, columns = atm_hbm.shape
    ocn_levels = ocn_ref.shape[1]
    atm_copies = tile_copies(atm_hbm, each(atm_ref), atm_sems)
    for copy in atm_copies:
        copy.start()
    even = lax.rem(lax.axis_index("tile"), 2) == 0
    quarter = tiles // 2

    @pl.when(even)
    def _():
        for place, ref in enumerate([outer_recv_ref, outer_ref, inner_ref, inner_recv_ref]):
            padded_ref[place * quarter : (place + 1) * quarter] = ref[...]

    @pl.when(jnp.logical_not(even))
    def _():
        for place, ref in enumerate([inner_recv_ref, inner_ref, outer_ref, outer_recv_ref]):
            padded_ref[place * quarter : (place + 1) * quarter] = ref[...]

    group = 16
    sub = lax.broadcasted_iota(jnp.int32, (group, columns), 0)
    row = lax.broadcasted_iota(jnp.int32, (columns, columns), 0)
    col = lax.broadcasted_iota(jnp.int32, (columns, columns), 1)

    def class_weight(number):
        weight = jnp.float32(0.0)
        for value, factor in enumerate(CLASS_TABLE):
            weight = jnp.where(number == value, jnp.float32(factor), weight)
        return weight

    def taper(spread):
        scaled = (row - col).astype(F32) * (1.0 / spread)
        return jnp.exp(-0.5 * scaled * scaled)

    stores = [
        pltpu.make_async_copy(atm_out_ref, atm_out_hbm, out_sems.at[0]),
        pltpu.make_async_copy(ocn_out_ref, ocn_out_hbm, out_sems.at[1]),
    ]
    parts = [
        ([tile_ref] + each(atm_ref), atm_out_ref, atm_pair_ref, atm_class_ref, atm_levels, ATM_SPREAD),
        (each(ocn_ref), ocn_out_ref, ocn_pair_ref, ocn_class_ref, ocn_levels, OCN_SPREAD),
    ]

    def weights(which):
        _, _, _, class_ref, _, width = parts[which]
        tapering = taper(width)
        for t in range(tiles):
            spread = jnp.zeros((members, columns), F32)
            for offset in range(2 * HALO + 1):
                spread = spread + class_weight(class_ref[t, offset]) * padded_ref[t + offset, which]
            vert = lax.dot_general(
                tapering, spread, NT, precision=lax.Precision.HIGHEST, preferred_element_type=F32
            ).astype(BF16)
            vert_ref[which, t] = vert
            column_ref[which, t] = vert.astype(F32).T

    def apply(which, t):
        refs, out_ref, pair_ref, _, levels, _ = parts[which]
        ref = refs[t]
        surface = [(levels - KA + i, RISE[i]) for i in range(KA)] if which == 0 else list(enumerate(FALL))
        coupling = dict(surface)
        paired = pair_ref[:, t * columns : (t + 1) * columns]
        for start in range(0, levels, group):
            count = min(group, levels - start)
            plain = [j for j in range(count) if start + j not in coupling]
            total = jnp.zeros((group, columns), F32)
            if plain:
                right = jnp.concatenate([ref[start + j] for j in plain], axis=1)
                product = jnp.dot(
                    vert_ref[which, t, start : start + group, :], right, preferred_element_type=F32
                )
                for place, j in enumerate(plain):
                    part = product[:, place * columns : (place + 1) * columns]
                    total = part if place == 0 else jnp.where(sub == j, part, total)
            for j in range(count):
                level = start + j
                if level in coupling:
                    column = jnp.broadcast_to(
                        column_ref[which, t, :, level : level + 1], (members, columns)
                    )
                    factor = column + paired * (COUPLING * coupling[level])
                    term = jnp.sum(ref[level].astype(F32) * factor, axis=0, keepdims=True)
                    total = jnp.where(sub == j, term, total)
            if which == 1:
                total = total * sea_ref[t].astype(F32)
            out_ref[start : start + count, t, :] = total[:count]

    def finish(which):
        stores[which].start()

    weights(1)
    weights(0)
    for t in range(tiles):
        apply(1, t)
    finish(1)
    apply(0, 0)
    for t in range(1, tiles):
        atm_copies[t - 1].wait()
        apply(0, t)
    finish(0)
    for store in stores:
        store.wait()


def pair_kernel(
    per_peer,
    pairing_ref,
    recv_ref,
    ocn_hbm,
    atm_pair_ref,
    ocn_pair_ref,
    ocn_ref,
    sems,
):
    tiles, _, members, columns = ocn_hbm.shape
    ocn_copies = tile_copies(ocn_hbm, each(ocn_ref), sems)
    for copy in ocn_copies:
        copy.start()
    peers, count = recv_ref.shape[0], recv_ref.shape[1] // 2

    def pair_columns(first, slots):
        rows = recv_ref[:, first : first + count, :].reshape(peers * count, members)
        return lax.dot_general(rows, slots, TN, preferred_element_type=F32)

    atm_pair_ref[...] = pair_columns(count, atm_slots(pairing_ref, columns, tiles, per_peer))
    ocn_pair_ref[...] = pair_columns(0, ocn_slots(columns, tiles, per_peer))
    for copy in ocn_copies:
        copy.wait()


def local(atm_anom, ocn_anom, atm_vec, ocn_vec, atm_to_ocean, sea_tiles, atm_class, ocn_class):
    tiles, members, atm_levels, columns = atm_anom.shape
    ocn_levels = ocn_anom.shape[2]
    axes = ("dom", "tile")
    devices = lax.axis_size("dom") * lax.axis_size("tile")
    per_peer = columns // devices
    peer_rows = tiles * per_peer

    by_level = (0, 2, 1, 3)
    atm = jnp.transpose(atm_anom, by_level)
    ocn = jnp.transpose(ocn_anom, by_level)
    atm_rows = jnp.transpose(atm_vec, (1, 0, 2))
    ocn_rows = jnp.transpose(ocn_vec, (1, 0, 2))
    params = pltpu.CompilerParams(vmem_limit_bytes=58 * MIB)

    elements = tiles * members * columns * (atm_levels + ocn_levels)
    top_elements = tiles * members * columns * (KA + KO)
    rest_shape = (tiles - 1,) + atm.shape[1:]
    tops = [
        pltpu.VMEM((tiles - 1, KA, members, columns), BF16),
        pltpu.VMEM((tiles, KO, members, columns), BF16),
        pltpu.SemaphoreType.DMA((2, tiles)),
    ]
    wholes = [pltpu.VMEM(rest_shape, BF16), pltpu.VMEM(ocn.shape, BF16)]
    whole_sems = [pltpu.SemaphoreType.DMA((tiles,)), pltpu.SemaphoreType.DMA((tiles,))]

    def cost(flops, count):
        return pl.CostEstimate(flops=flops, bytes_accessed=2 * count, transcendentals=0)

    outgoing, tile, tile_vec = pl.pallas_call(
        functools.partial(project_kernel, per_peer),
        out_shape=[
            jax.ShapeDtypeStruct((devices, 2 * peer_rows, members), BF16),
            pltpu.VMEM((atm_levels, members, columns), BF16),
            pltpu.VMEM((columns, columns), F32),
        ],
        in_specs=[ANY_SPEC] * 6,
        out_specs=[VMEM_SPEC] * 3,
        scratch_shapes=tops
        + [
            pltpu.SMEM(sea_tiles.shape, jnp.int32),
            pltpu.VMEM(atm_to_ocean.shape, jnp.int32),
            pltpu.VMEM(atm_rows.shape, BF16),
            pltpu.VMEM((KO, tiles, columns), BF16),
            pltpu.SemaphoreType.DMA((5,)),
        ],
        compiler_params=params,
        cost_estimate=cost(4 * top_elements, top_elements),
        name="project",
    )(sea_tiles, atm_to_ocean, atm_rows, ocn_rows, atm, ocn)
    incoming = lax.all_to_all(outgoing, axes, split_axis=0, concat_axis=0, tiled=True)

    edge = pltpu.VMEM((tiles // 2, 2, members, columns), F32)
    inner, outer = pl.pallas_call(
        first_kernel,
        out_shape=[edge, edge],
        in_specs=[ANY_SPEC] * 3 + [VMEM_SPEC] * 2 + [ANY_SPEC] * 2,
        out_specs=[VMEM_SPEC] * 2,
        scratch_shapes=wholes
        + [
            pltpu.SMEM(sea_tiles.shape, jnp.int32),
            pltpu.VMEM(atm_rows.shape, BF16),
            pltpu.VMEM(ocn_rows.shape, BF16),
            pltpu.VMEM((2 * tiles, columns, columns), F32),
            pltpu.VMEM((2 * tiles, 2 * columns, 2 * columns), BF16),
            pltpu.VMEM((tiles, 2, members, columns), F32),
            pltpu.SemaphoreType.DMA((3,)),
        ]
        + whole_sems,
        compiler_params=params,
        cost_estimate=cost(2 * 256 * elements, elements),
        name="first_pass",
    )(sea_tiles, atm_rows, ocn_rows, in_vmem(tile), in_vmem(tile_vec), atm, ocn)

    count = lax.axis_size("tile")
    outer_pairs = [(i, (i + 1) % count if i % 2 else (i - 1) % count) for i in range(count)]
    outer_recv = lax.ppermute(outer, "tile", outer_pairs)
    inner_recv = lax.ppermute(inner, "tile", [(i, i ^ 1) for i in range(count)])

    pair = pltpu.VMEM((members, tiles * columns), F32)
    atm_pair, ocn_pair, ocn_v = pl.pallas_call(
        functools.partial(pair_kernel, per_peer),
        out_shape=[pair, pair, pltpu.VMEM(ocn.shape, BF16)],
        in_specs=[VMEM_SPEC, VMEM_SPEC, ANY_SPEC],
        out_specs=[VMEM_SPEC] * 3,
        scratch_shapes=[pltpu.SemaphoreType.DMA((tiles,))],
        compiler_params=pltpu.CompilerParams(vmem_limit_bytes=52 * MIB),
        cost_estimate=cost(40 * top_elements, 4 * top_elements),
        name="pair_columns",
    )(atm_to_ocean, in_vmem(incoming), ocn)

    atm_out, ocn_out = pl.pallas_call(
        second_kernel,
        out_shape=[
            jax.ShapeDtypeStruct((atm_levels, tiles, columns), F32),
            jax.ShapeDtypeStruct((ocn_levels, tiles, columns), F32),
        ],
        in_specs=[SMEM_SPEC] * 3 + [VMEM_SPEC] * 8 + [ANY_SPEC],
        out_specs=[ANY_SPEC] * 2,
        scratch_shapes=[
            pltpu.VMEM(rest_shape, BF16),
            pltpu.VMEM((atm_levels, tiles, columns), F32),
            pltpu.VMEM((ocn_levels, tiles, columns), F32),
            pltpu.VMEM((2 * tiles, 2, members, columns), F32),
            pltpu.VMEM((2, tiles, columns, members), BF16),
            pltpu.VMEM((2, tiles, members, columns), F32),
            pltpu.SemaphoreType.DMA((2,)),
            pltpu.SemaphoreType.DMA((tiles,)),
        ],
        compiler_params=pltpu.CompilerParams(vmem_limit_bytes=50 * MIB),
        cost_estimate=cost(2 * 256 * elements, elements),
        name="second_pass",
    )(
        sea_tiles,
        atm_class,
        ocn_class,
        in_vmem(inner),
        in_vmem(outer),
        in_vmem(inner_recv),
        in_vmem(outer_recv),
        in_vmem(atm_pair),
        in_vmem(ocn_pair),
        in_vmem(ocn_v),
        in_vmem(tile),
        atm,
    )
    return jnp.transpose(atm_out, (1, 0, 2)), jnp.transpose(ocn_out, (1, 0, 2))


def solution(mesh):
    in_specs = (
        P(("dom", "tile"), None, None, None),
        P(("dom", "tile"), None, None, None),
        P(("dom", "tile"), None, None),
        P(("dom", "tile"), None, None),
        P(("dom", "tile"), None),
        P(("dom", "tile")),
        P(("dom", "tile"), None),
        P(("dom", "tile"), None),
    )
    out_specs = (P(("dom", "tile"), None, None), P(("dom", "tile"), None, None))
    return jax.shard_map(local, mesh=mesh, in_specs=in_specs, out_specs=out_specs, check_vma=False)
```

```python
import functools
import math

import jax
import jax.numpy as jnp
from jax import lax
from jax.experimental import pallas as pl
from jax.experimental.pallas import tpu as pltpu
from jax.sharding import PartitionSpec as P

KA = 16
KO = 16
HALO = 2
GROUP = 4
VECTOR_LEVELS = (31, 19)
REGIONS = [[(0, 0)], [(0, 1), (0, 2)], [(0, 3), (1, 0)], [(1, 1), (1, 2), (1, 3)]]

COUPLING = 8.0
ATM_SPREAD = 12.0
OCN_SPREAD = 8.0
CLASS_TABLE = (1.0, 0.7, 0.45, 0.25, 0.0)

BF16 = jnp.bfloat16
F32 = jnp.float32
MIB = 1 << 20
NT = (((1,), (1,)), ((), ()))
TN = (((0,), (0,)), ((), ()))
VMEM_SPEC = pl.BlockSpec(memory_space=pltpu.VMEM)
SMEM_SPEC = pl.BlockSpec(memory_space=pltpu.SMEM)
ANY_SPEC = pl.BlockSpec(memory_space=pl.ANY)

RISE = [math.exp(-2.0 * (KA - 1 - s) / KA) for s in range(KA)]
FALL = [math.exp(-2.0 * o / KO) for o in range(KO)]


def slot_rows(index, columns, tiles, per_peer):
    tile, column = index // columns, index % columns
    return (tile // tiles) * (tiles * per_peer) + (tile % tiles) * per_peer + column % per_peer


def one_hot(rows, width):
    position = lax.broadcasted_iota(jnp.int32, (width, rows.shape[1]), 0)
    return jnp.where(position == rows, 1.0, 0.0).astype(BF16)


def atm_slots(pairing_ref, columns, tiles, per_peer):
    index = jnp.concatenate([pairing_ref[t : t + 1, :] for t in range(tiles)], axis=1)
    return one_hot(slot_rows(index, columns, tiles, per_peer), tiles * columns)


def ocn_slots(columns, tiles, per_peer):
    place = lax.broadcasted_iota(jnp.int32, (1, tiles * columns), 1)
    tile, column = place // columns, place % columns
    rows = (column // per_peer) * (tiles * per_peer) + tile * per_peer + column % per_peer
    return one_hot(rows, tiles * columns)


def in_vmem(array):
    return pltpu.with_memory_space_constraint(array, pltpu.VMEM)


def tile_copies(source, targets, sems):
    first = source.shape[0] - len(targets)
    return [
        pltpu.make_async_copy(source.at[first + i], target, sems.at[i])
        for i, target in enumerate(targets)
    ]


def each(ref):
    return [ref.at[i] for i in range(ref.shape[0])]


def spread_vectors(source, vec_ref, which, tiles):
    levels, _, columns = source.shape
    for t in range(tiles):
        place = which * tiles + t
        vec_ref[place, :levels] = source[:, t, :].astype(F32)
        if levels < columns:
            vec_ref[place, levels:] = jnp.zeros((columns - levels, columns), F32)


def project_kernel(
    per_peer,
    sea_hbm,
    pairing_hbm,
    atm_vec_hbm,
    ocn_vec_hbm,
    atm_hbm,
    ocn_hbm,
    send_ref,
    tile_ref,
    tile_vec_ref,
    atm_top,
    ocn_top,
    sems,
    sea_ref,
    pairing_ref,
    atm_vec_ref,
    ocn_vec_ref,
    small_sems,
):
    tiles, atm_levels, members, columns = atm_hbm.shape
    start = atm_levels - KA
    peers, count = send_ref.shape[0], send_ref.shape[1] // 2
    small = [
        pltpu.make_async_copy(pairing_hbm, pairing_ref, small_sems.at[0]),
        pltpu.make_async_copy(atm_vec_hbm, atm_vec_ref, small_sems.at[1]),
        pltpu.make_async_copy(ocn_vec_hbm.at[pl.ds(0, KO)], ocn_vec_ref, small_sems.at[2]),
        pltpu.make_async_copy(sea_hbm, sea_ref, small_sems.at[3]),
    ]
    for load in small:
        load.start()
    atm_tops = [tile_ref.at[pl.ds(start, KA)]] + [atm_top.at[t] for t in range(tiles - 1)]
    loads = [
        [
            pltpu.make_async_copy(atm_hbm.at[t, pl.ds(start, KA)], atm_tops[t], sems.at[0, t]),
            pltpu.make_async_copy(ocn_hbm.at[t, pl.ds(0, KO)], ocn_top.at[t], sems.at[1, t]),
        ]
        for t in range(tiles)
    ]
    for pair in loads:
        for load in pair:
            load.start()
    rest = pltpu.make_async_copy(
        atm_hbm.at[0, pl.ds(0, start)], tile_ref.at[pl.ds(0, start)], small_sems.at[4]
    )
    rest.start()
    for load in small:
        load.wait()
    slots = [
        atm_slots(pairing_ref, columns, tiles, per_peer),
        ocn_slots(columns, tiles, per_peer),
    ]
    atm_rows = atm_vec_ref[start : start + KA].astype(F32)
    ocn_rows = ocn_vec_ref[...].astype(F32)
    tile_vec_ref[:atm_levels] = atm_vec_ref[:, 0, :].astype(F32)
    if atm_levels < columns:
        tile_vec_ref[atm_levels:] = jnp.zeros((columns - atm_levels, columns), F32)

    def projection(top, t, rows, weights):
        total = jnp.zeros((members, columns), F32)
        for s, weight in enumerate(weights):
            total = total + top[s].astype(F32) * (rows[s, t : t + 1, :] * weight)
        return total

    atm_proj, ocn_proj = [], []
    for t in range(tiles):
        for load in loads[t]:
            load.wait()
        atm_proj.append(projection(atm_tops[t], t, atm_rows, RISE).astype(BF16))
        sea = sea_ref[t].astype(F32)
        ocn_proj.append((projection(ocn_top.at[t], t, ocn_rows, FALL) * sea).astype(BF16))
    for place, proj in enumerate([atm_proj, ocn_proj]):
        rows = lax.dot_general(
            slots[place], jnp.concatenate(proj, axis=1), NT, preferred_element_type=F32
        ).astype(BF16)
        send_ref[:, place * count : (place + 1) * count, :] = rows.reshape(peers, count, members)
    rest.wait()


def first_kernel(
    sea_hbm,
    atm_vec_hbm,
    ocn_vec_hbm,
    tile_ref,
    tile_vec_ref,
    atm_hbm,
    ocn_hbm,
    inner_ref,
    outer_ref,
    atm_ref,
    ocn_ref,
    sea_ref,
    atm_vec_ref,
    ocn_vec_ref,
    vec_ref,
    weight_ref,
    coeff_ref,
    small_sems,
    atm_sems,
    ocn_sems,
):
    tiles, atm_levels, members, columns = atm_hbm.shape
    ocn_levels = ocn_hbm.shape[1]
    small = [
        pltpu.make_async_copy(atm_vec_hbm, atm_vec_ref, small_sems.at[0]),
        pltpu.make_async_copy(ocn_vec_hbm, ocn_vec_ref, small_sems.at[1]),
        pltpu.make_async_copy(sea_hbm, sea_ref, small_sems.at[2]),
    ]
    for load in small:
        load.start()
    atm_copies = tile_copies(atm_hbm, each(atm_ref), atm_sems)
    ocn_copies = tile_copies(ocn_hbm, each(ocn_ref), ocn_sems)
    copies = [[None] + atm_copies, ocn_copies]
    held = [[tile_ref] + each(atm_ref), each(ocn_ref)]
    for region in REGIONS[1:3]:
        for which, t in region:
            copies[which][t].start()
    even = lax.rem(lax.axis_index("tile"), 2) == 0
    lane = lax.broadcasted_iota(jnp.int32, (members, columns), 1)

    zeros = jnp.zeros((columns, columns), BF16)

    def transpose_vectors(place):
        vec_t = vec_ref[place].T.astype(BF16)
        weight_ref[place, :columns, :columns] = vec_t
        weight_ref[place, :columns, columns:] = zeros
        weight_ref[place, columns:, :columns] = zeros
        weight_ref[place, columns:, columns:] = vec_t

    def coefficients(ref, place, levels):
        vector_levels = VECTOR_LEVELS[place // tiles]
        levels = levels - vector_levels
        half = (levels + 1) // 2
        second = levels - half
        total = jnp.zeros((members, columns), F32)
        for first in range(0, half, GROUP):
            count = min(GROUP, half - first)
            left = ref[first : first + count].reshape(count * members, columns)
            right = ref[second + first : second + first + count].reshape(count * members, columns)
            product = jnp.dot(
                jnp.concatenate([left, right], axis=1),
                weight_ref[place],
                preferred_element_type=F32,
            )
            for j in range(count):
                part = product[j * members : (j + 1) * members]
                total = jnp.where(lane == first + j, part[:, :columns], total)
                total = jnp.where(lane == second + first + j, part[:, columns:], total)
        for level in range(levels, levels + vector_levels):
            product = ref[level].astype(F32) * vec_ref[place, level : level + 1, :]
            total = jnp.where(lane == level, jnp.sum(product, axis=1, keepdims=True), total)
        return total

    level_counts = [atm_levels, ocn_levels]
    vec_ref[0] = tile_vec_ref[...]
    transpose_vectors(0)
    for number, region in enumerate(REGIONS):
        if number == 1:
            for load in small:
                load.wait()
            spread_vectors(atm_vec_ref, vec_ref, 0, tiles)
            spread_vectors(ocn_vec_ref, vec_ref, 1, tiles)
            for place in range(1, 2 * tiles):
                transpose_vectors(place)
        for which, t in region:
            if copies[which][t] is not None:
                copies[which][t].wait()
        for later in REGIONS[max(number + 2, 3) : number + 3]:
            for which, t in later:
                copies[which][t].start()
        for which, t in region:
            total = coefficients(held[which][t], which * tiles + t, level_counts[which])
            if which == 1:
                total = total * sea_ref[t].astype(F32)
            coeff_ref[t, which] = total
    half = tiles // 2
    low, high = coeff_ref[:half], coeff_ref[half:]
    inner_ref[...] = jnp.where(even, high, low)
    outer_ref[...] = jnp.where(even, low, high)


def second_kernel(
    sea_ref,
    atm_class_ref,
    ocn_class_ref,
    inner_ref,
    outer_ref,
    inner_recv_ref,
    outer_recv_ref,
    atm_pair_ref,
    ocn_pair_ref,
    ocn_ref,
    tile_ref,
    next_ref,
    atm_hbm,
    atm_out_hbm,
    ocn_out_hbm,
    atm_ref,
    atm_out_ref,
    ocn_out_ref,
    padded_ref,
    vert_ref,
    column_ref,
    out_sems,
    atm_sems,
):
    tiles, atm_levels, members, columns = atm_hbm.shape
    ocn_levels = ocn_ref.shape[1]
    atm_copies = tile_copies(atm_hbm, each(atm_ref), atm_sems)
    for copy in atm_copies:
        copy.start()
    even = lax.rem(lax.axis_index("tile"), 2) == 0
    quarter = tiles // 2

    @pl.when(even)
    def _():
        for place, ref in enumerate([outer_recv_ref, outer_ref, inner_ref, inner_recv_ref]):
            padded_ref[place * quarter : (place + 1) * quarter] = ref[...]

    @pl.when(jnp.logical_not(even))
    def _():
        for place, ref in enumerate([inner_recv_ref, inner_ref, outer_ref, outer_recv_ref]):
            padded_ref[place * quarter : (place + 1) * quarter] = ref[...]

    group = 16
    sub = lax.broadcasted_iota(jnp.int32, (group, columns), 0)
    row = lax.broadcasted_iota(jnp.int32, (columns, columns), 0)
    col = lax.broadcasted_iota(jnp.int32, (columns, columns), 1)

    def class_weight(number):
        weight = jnp.float32(0.0)
        for value, factor in enumerate(CLASS_TABLE):
            weight = jnp.where(number == value, jnp.float32(factor), weight)
        return weight

    def taper(spread):
        scaled = (row - col).astype(F32) * (1.0 / spread)
        return jnp.exp(-0.5 * scaled * scaled)

    stores = [
        pltpu.make_async_copy(atm_out_ref, atm_out_hbm, out_sems.at[0]),
        pltpu.make_async_copy(ocn_out_ref, ocn_out_hbm, out_sems.at[1]),
    ]
    parts = [
        ([tile_ref, next_ref] + each(atm_ref), atm_out_ref, atm_pair_ref, atm_class_ref, atm_levels, ATM_SPREAD),
        (each(ocn_ref), ocn_out_ref, ocn_pair_ref, ocn_class_ref, ocn_levels, OCN_SPREAD),
    ]

    def weights(which):
        _, _, _, class_ref, _, width = parts[which]
        tapering = taper(width)
        for t in range(tiles):
            spread = jnp.zeros((members, columns), F32)
            for offset in range(2 * HALO + 1):
                spread = spread + class_weight(class_ref[t, offset]) * padded_ref[t + offset, which]
            vert = lax.dot_general(
                tapering, spread, NT, precision=lax.Precision.HIGHEST, preferred_element_type=F32
            ).astype(BF16)
            vert_ref[which, t] = vert
            column_ref[which, t] = vert.astype(F32).T

    def apply(which, t):
        refs, out_ref, pair_ref, _, levels, _ = parts[which]
        ref = refs[t]
        surface = [(levels - KA + i, RISE[i]) for i in range(KA)] if which == 0 else list(enumerate(FALL))
        coupling = dict(surface)
        paired = pair_ref[:, t * columns : (t + 1) * columns]
        for start in range(0, levels, group):
            count = min(group, levels - start)
            plain = [j for j in range(count) if start + j not in coupling]
            total = jnp.zeros((group, columns), F32)
            if plain:
                right = jnp.concatenate([ref[start + j] for j in plain], axis=1)
                product = jnp.dot(
                    vert_ref[which, t, start : start + group, :], right, preferred_element_type=F32
                )
                for place, j in enumerate(plain):
                    part = product[:, place * columns : (place + 1) * columns]
                    total = part if place == 0 else jnp.where(sub == j, part, total)
            for j in range(count):
                level = start + j
                if level in coupling:
                    column = jnp.broadcast_to(
                        column_ref[which, t, :, level : level + 1], (members, columns)
                    )
                    factor = column + paired * (COUPLING * coupling[level])
                    term = jnp.sum(ref[level].astype(F32) * factor, axis=0, keepdims=True)
                    total = jnp.where(sub == j, term, total)
            if which == 1:
                total = total * sea_ref[t].astype(F32)
            out_ref[start : start + count, t, :] = total[:count]

    def finish(which):
        stores[which].start()

    weights(1)
    weights(0)
    for t in range(tiles):
        apply(1, t)
    finish(1)
    apply(0, 0)
    apply(0, 1)
    for t in range(2, tiles):
        atm_copies[t - 2].wait()
        apply(0, t)
    finish(0)
    for store in stores:
        store.wait()


def pair_kernel(
    per_peer,
    pairing_ref,
    recv_ref,
    ocn_hbm,
    atm_hbm,
    atm_pair_ref,
    ocn_pair_ref,
    ocn_ref,
    next_ref,
    sems,
):
    tiles, _, members, columns = ocn_hbm.shape
    copies = tile_copies(ocn_hbm, each(ocn_ref), sems)
    copies.append(pltpu.make_async_copy(atm_hbm.at[1], next_ref, sems.at[tiles]))
    for copy in copies:
        copy.start()
    peers, count = recv_ref.shape[0], recv_ref.shape[1] // 2

    def pair_columns(first, slots):
        rows = recv_ref[:, first : first + count, :].reshape(peers * count, members)
        return lax.dot_general(rows, slots, TN, preferred_element_type=F32)

    atm_pair_ref[...] = pair_columns(count, atm_slots(pairing_ref, columns, tiles, per_peer))
    ocn_pair_ref[...] = pair_columns(0, ocn_slots(columns, tiles, per_peer))
    for copy in copies:
        copy.wait()


def local(atm_anom, ocn_anom, atm_vec, ocn_vec, atm_to_ocean, sea_tiles, atm_class, ocn_class):
    tiles, members, atm_levels, columns = atm_anom.shape
    ocn_levels = ocn_anom.shape[2]
    axes = ("dom", "tile")
    devices = lax.axis_size("dom") * lax.axis_size("tile")
    per_peer = columns // devices
    peer_rows = tiles * per_peer

    by_level = (0, 2, 1, 3)
    atm = jnp.transpose(atm_anom, by_level)
    ocn = jnp.transpose(ocn_anom, by_level)
    atm_rows = jnp.transpose(atm_vec, (1, 0, 2))
    ocn_rows = jnp.transpose(ocn_vec, (1, 0, 2))
    params = pltpu.CompilerParams(vmem_limit_bytes=58 * MIB)

    elements = tiles * members * columns * (atm_levels + ocn_levels)
    top_elements = tiles * members * columns * (KA + KO)
    rest_shape = (tiles - 1,) + atm.shape[1:]
    tops = [
        pltpu.VMEM((tiles - 1, KA, members, columns), BF16),
        pltpu.VMEM((tiles, KO, members, columns), BF16),
        pltpu.SemaphoreType.DMA((2, tiles)),
    ]
    wholes = [pltpu.VMEM(rest_shape, BF16), pltpu.VMEM(ocn.shape, BF16)]
    whole_sems = [pltpu.SemaphoreType.DMA((tiles,)), pltpu.SemaphoreType.DMA((tiles,))]

    def cost(flops, count):
        return pl.CostEstimate(flops=flops, bytes_accessed=2 * count, transcendentals=0)

    outgoing, tile, tile_vec = pl.pallas_call(
        functools.partial(project_kernel, per_peer),
        out_shape=[
            jax.ShapeDtypeStruct((devices, 2 * peer_rows, members), BF16),
            pltpu.VMEM((atm_levels, members, columns), BF16),
            pltpu.VMEM((columns, columns), F32),
        ],
        in_specs=[ANY_SPEC] * 6,
        out_specs=[VMEM_SPEC] * 3,
        scratch_shapes=tops
        + [
            pltpu.SMEM(sea_tiles.shape, jnp.int32),
            pltpu.VMEM(atm_to_ocean.shape, jnp.int32),
            pltpu.VMEM(atm_rows.shape, BF16),
            pltpu.VMEM((KO, tiles, columns), BF16),
            pltpu.SemaphoreType.DMA((5,)),
        ],
        compiler_params=params,
        cost_estimate=cost(4 * top_elements, top_elements),
        name="project",
    )(sea_tiles, atm_to_ocean, atm_rows, ocn_rows, atm, ocn)
    incoming = lax.all_to_all(outgoing, axes, split_axis=0, concat_axis=0, tiled=True)

    edge = pltpu.VMEM((tiles // 2, 2, members, columns), F32)
    inner, outer = pl.pallas_call(
        first_kernel,
        out_shape=[edge, edge],
        in_specs=[ANY_SPEC] * 3 + [VMEM_SPEC] * 2 + [ANY_SPEC] * 2,
        out_specs=[VMEM_SPEC] * 2,
        scratch_shapes=wholes
        + [
            pltpu.SMEM(sea_tiles.shape, jnp.int32),
            pltpu.VMEM(atm_rows.shape, BF16),
            pltpu.VMEM(ocn_rows.shape, BF16),
            pltpu.VMEM((2 * tiles, columns, columns), F32),
            pltpu.VMEM((2 * tiles, 2 * columns, 2 * columns), BF16),
            pltpu.VMEM((tiles, 2, members, columns), F32),
            pltpu.SemaphoreType.DMA((3,)),
        ]
        + whole_sems,
        compiler_params=params,
        cost_estimate=cost(2 * 256 * elements, elements),
        name="first_pass",
    )(sea_tiles, atm_rows, ocn_rows, in_vmem(tile), in_vmem(tile_vec), atm, ocn)

    count = lax.axis_size("tile")
    outer_pairs = [(i, (i + 1) % count if i % 2 else (i - 1) % count) for i in range(count)]
    outer_recv = lax.ppermute(outer, "tile", outer_pairs)
    inner_recv = lax.ppermute(inner, "tile", [(i, i ^ 1) for i in range(count)])

    pair = pltpu.VMEM((members, tiles * columns), F32)
    atm_pair, ocn_pair, ocn_v, next_tile = pl.pallas_call(
        functools.partial(pair_kernel, per_peer),
        out_shape=[
            pair,
            pair,
            pltpu.VMEM(ocn.shape, BF16),
            pltpu.VMEM((atm_levels, members, columns), BF16),
        ],
        in_specs=[VMEM_SPEC, VMEM_SPEC, ANY_SPEC, ANY_SPEC],
        out_specs=[VMEM_SPEC] * 4,
        scratch_shapes=[pltpu.SemaphoreType.DMA((tiles + 1,))],
        compiler_params=pltpu.CompilerParams(vmem_limit_bytes=44 * MIB),
        cost_estimate=cost(40 * top_elements, 4 * top_elements),
        name="pair_columns",
    )(atm_to_ocean, in_vmem(incoming), ocn, atm)

    atm_out, ocn_out = pl.pallas_call(
        second_kernel,
        out_shape=[
            jax.ShapeDtypeStruct((atm_levels, tiles, columns), F32),
            jax.ShapeDtypeStruct((ocn_levels, tiles, columns), F32),
        ],
        in_specs=[SMEM_SPEC] * 3 + [VMEM_SPEC] * 9 + [ANY_SPEC],
        out_specs=[ANY_SPEC] * 2,
        scratch_shapes=[
            pltpu.VMEM((tiles - 2,) + atm.shape[1:], BF16),
            pltpu.VMEM((atm_levels, tiles, columns), F32),
            pltpu.VMEM((ocn_levels, tiles, columns), F32),
            pltpu.VMEM((2 * tiles, 2, members, columns), F32),
            pltpu.VMEM((2, tiles, columns, members), BF16),
            pltpu.VMEM((2, tiles, members, columns), F32),
            pltpu.SemaphoreType.DMA((2,)),
            pltpu.SemaphoreType.DMA((tiles,)),
        ],
        compiler_params=pltpu.CompilerParams(vmem_limit_bytes=42 * MIB),
        cost_estimate=cost(2 * 256 * elements, elements),
        name="second_pass",
    )(
        sea_tiles,
        atm_class,
        ocn_class,
        in_vmem(inner),
        in_vmem(outer),
        in_vmem(inner_recv),
        in_vmem(outer_recv),
        in_vmem(atm_pair),
        in_vmem(ocn_pair),
        in_vmem(ocn_v),
        in_vmem(tile),
        in_vmem(next_tile),
        atm,
    )
    return jnp.transpose(atm_out, (1, 0, 2)), jnp.transpose(ocn_out, (1, 0, 2))


def solution(mesh):
    in_specs = (
        P(("dom", "tile"), None, None, None),
        P(("dom", "tile"), None, None, None),
        P(("dom", "tile"), None, None),
        P(("dom", "tile"), None, None),
        P(("dom", "tile"), None),
        P(("dom", "tile")),
        P(("dom", "tile"), None),
        P(("dom", "tile"), None),
    )
    out_specs = (P(("dom", "tile"), None, None), P(("dom", "tile"), None, None))
    return jax.shard_map(local, mesh=mesh, in_specs=in_specs, out_specs=out_specs, check_vma=False)
```

```python
import functools
import math

import jax
import jax.numpy as jnp
from jax import lax
from jax.experimental import pallas as pl
from jax.experimental.pallas import tpu as pltpu
from jax.sharding import PartitionSpec as P

KA = 16
KO = 16
HALO = 2
GROUP = 4
VECTOR_LEVELS = (31, 19)
REGIONS = [[(0, 0)], [(0, 1)], [(0, 2), (0, 3)], [(1, 0), (1, 1)], [(1, 2), (1, 3)]]

COUPLING = 8.0
ATM_SPREAD = 12.0
OCN_SPREAD = 8.0
CLASS_TABLE = (1.0, 0.7, 0.45, 0.25, 0.0)

BF16 = jnp.bfloat16
F32 = jnp.float32
MIB = 1 << 20
NT = (((1,), (1,)), ((), ()))
TN = (((0,), (0,)), ((), ()))
VMEM_SPEC = pl.BlockSpec(memory_space=pltpu.VMEM)
SMEM_SPEC = pl.BlockSpec(memory_space=pltpu.SMEM)
ANY_SPEC = pl.BlockSpec(memory_space=pl.ANY)

RISE = [math.exp(-2.0 * (KA - 1 - s) / KA) for s in range(KA)]
FALL = [math.exp(-2.0 * o / KO) for o in range(KO)]


def slot_rows(index, columns, tiles, per_peer):
    tile, column = index // columns, index % columns
    return (tile // tiles) * (tiles * per_peer) + (tile % tiles) * per_peer + column % per_peer


def one_hot(rows, width):
    position = lax.broadcasted_iota(jnp.int32, (width, rows.shape[1]), 0)
    return jnp.where(position == rows, 1.0, 0.0).astype(BF16)


def atm_slots(pairing_ref, columns, tiles, per_peer):
    index = jnp.concatenate([pairing_ref[t : t + 1, :] for t in range(tiles)], axis=1)
    return one_hot(slot_rows(index, columns, tiles, per_peer), tiles * columns)


def ocn_slots(columns, tiles, per_peer):
    place = lax.broadcasted_iota(jnp.int32, (1, tiles * columns), 1)
    tile, column = place // columns, place % columns
    rows = (column // per_peer) * (tiles * per_peer) + tile * per_peer + column % per_peer
    return one_hot(rows, tiles * columns)


def in_vmem(array):
    return pltpu.with_memory_space_constraint(array, pltpu.VMEM)


def tile_copies(source, targets, sems):
    first = source.shape[0] - len(targets)
    return [
        pltpu.make_async_copy(source.at[first + i], target, sems.at[i])
        for i, target in enumerate(targets)
    ]


def each(ref):
    return [ref.at[i] for i in range(ref.shape[0])]


def spread_vectors(source, vec_ref, which, tiles):
    levels, _, columns = source.shape
    for t in range(tiles):
        place = which * tiles + t
        vec_ref[place, :levels] = source[:, t, :].astype(F32)
        if levels < columns:
            vec_ref[place, levels:] = jnp.zeros((columns - levels, columns), F32)


def project_kernel(
    per_peer,
    sea_hbm,
    pairing_hbm,
    atm_vec_hbm,
    ocn_vec_hbm,
    atm_hbm,
    ocn_hbm,
    send_ref,
    tile_ref,
    tile_vec_ref,
    atm_top,
    ocn_top,
    sems,
    sea_ref,
    pairing_ref,
    atm_vec_ref,
    ocn_vec_ref,
    small_sems,
):
    tiles, atm_levels, members, columns = atm_hbm.shape
    start = atm_levels - KA
    peers, count = send_ref.shape[0], send_ref.shape[1] // 2
    small = [
        pltpu.make_async_copy(pairing_hbm, pairing_ref, small_sems.at[0]),
        pltpu.make_async_copy(atm_vec_hbm, atm_vec_ref, small_sems.at[1]),
        pltpu.make_async_copy(ocn_vec_hbm.at[pl.ds(0, KO)], ocn_vec_ref, small_sems.at[2]),
        pltpu.make_async_copy(sea_hbm, sea_ref, small_sems.at[3]),
    ]
    for load in small:
        load.start()
    atm_tops = [tile_ref.at[pl.ds(start, KA)]] + [atm_top.at[t] for t in range(tiles - 1)]
    loads = [
        [
            pltpu.make_async_copy(atm_hbm.at[t, pl.ds(start, KA)], atm_tops[t], sems.at[0, t]),
            pltpu.make_async_copy(ocn_hbm.at[t, pl.ds(0, KO)], ocn_top.at[t], sems.at[1, t]),
        ]
        for t in range(tiles)
    ]
    for place in range(2):
        for pair in loads:
            pair[place].start()
    rest = pltpu.make_async_copy(
        atm_hbm.at[0, pl.ds(0, start)], tile_ref.at[pl.ds(0, start)], small_sems.at[4]
    )
    rest.start()
    slots = [None, ocn_slots(columns, tiles, per_peer)]
    for load in small:
        load.wait()
    slots[0] = atm_slots(pairing_ref, columns, tiles, per_peer)
    atm_rows = atm_vec_ref[start : start + KA].astype(F32)
    ocn_rows = ocn_vec_ref[...].astype(F32)
    tile_vec_ref[:atm_levels] = atm_vec_ref[:, 0, :].astype(F32)
    if atm_levels < columns:
        tile_vec_ref[atm_levels:] = jnp.zeros((columns - atm_levels, columns), F32)

    def projection(top, t, rows, weights):
        total = jnp.zeros((members, columns), F32)
        for s, weight in enumerate(weights):
            total = total + top[s].astype(F32) * (rows[s, t : t + 1, :] * weight)
        return total

    def route(place, proj):
        rows = lax.dot_general(
            slots[place], jnp.concatenate(proj, axis=1), NT, preferred_element_type=F32
        ).astype(BF16)
        send_ref[:, place * count : (place + 1) * count, :] = rows.reshape(peers, count, members)

    for t in range(tiles):
        loads[t][0].wait()
    atm_proj = [
        projection(atm_tops[t], t, atm_rows, RISE).astype(BF16) for t in range(tiles)
    ]
    for t in range(tiles):
        loads[t][1].wait()
    route(0, atm_proj)
    ocn_proj = [
        (projection(ocn_top.at[t], t, ocn_rows, FALL) * sea_ref[t].astype(F32)).astype(BF16)
        for t in range(tiles)
    ]
    route(1, ocn_proj)
    rest.wait()


def first_kernel(
    sea_hbm,
    atm_vec_hbm,
    ocn_vec_hbm,
    tile_ref,
    tile_vec_ref,
    atm_hbm,
    ocn_hbm,
    inner_ref,
    outer_ref,
    atm_ref,
    ocn_ref,
    sea_ref,
    atm_vec_ref,
    ocn_vec_ref,
    vec_ref,
    weight_ref,
    coeff_ref,
    small_sems,
    atm_sems,
    ocn_sems,
):
    tiles, atm_levels, members, columns = atm_hbm.shape
    ocn_levels = ocn_hbm.shape[1]
    small = [
        pltpu.make_async_copy(atm_vec_hbm, atm_vec_ref, small_sems.at[0]),
        pltpu.make_async_copy(ocn_vec_hbm, ocn_vec_ref, small_sems.at[1]),
        pltpu.make_async_copy(sea_hbm, sea_ref, small_sems.at[2]),
    ]
    for load in small:
        load.start()
    atm_copies = tile_copies(atm_hbm, each(atm_ref), atm_sems)
    ocn_copies = tile_copies(ocn_hbm, each(ocn_ref), ocn_sems)
    copies = [[None] + atm_copies, ocn_copies]
    held = [[tile_ref] + each(atm_ref), each(ocn_ref)]
    for region in REGIONS[1:3]:
        for which, t in region:
            copies[which][t].start()
    even = lax.rem(lax.axis_index("tile"), 2) == 0
    lane = lax.broadcasted_iota(jnp.int32, (members, columns), 1)

    zeros = jnp.zeros((columns, columns), BF16)

    def transpose_vectors(place):
        vec_t = vec_ref[place].T.astype(BF16)
        weight_ref[place, :columns, :columns] = vec_t
        weight_ref[place, :columns, columns:] = zeros
        weight_ref[place, columns:, :columns] = zeros
        weight_ref[place, columns:, columns:] = vec_t

    def coefficients(ref, place, levels):
        vector_levels = VECTOR_LEVELS[place // tiles]
        levels = levels - vector_levels
        half = (levels + 1) // 2
        second = levels - half
        total = jnp.zeros((members, columns), F32)
        for first in range(0, half, GROUP):
            count = min(GROUP, half - first)
            left = ref[first : first + count].reshape(count * members, columns)
            right = ref[second + first : second + first + count].reshape(count * members, columns)
            product = jnp.dot(
                jnp.concatenate([left, right], axis=1),
                weight_ref[place],
                preferred_element_type=F32,
            )
            for j in range(count):
                part = product[j * members : (j + 1) * members]
                total = jnp.where(lane == first + j, part[:, :columns], total)
                total = jnp.where(lane == second + first + j, part[:, columns:], total)
        for level in range(levels, levels + vector_levels):
            product = ref[level].astype(F32) * vec_ref[place, level : level + 1, :]
            total = jnp.where(lane == level, jnp.sum(product, axis=1, keepdims=True), total)
        return total

    level_counts = [atm_levels, ocn_levels]
    vec_ref[0] = tile_vec_ref[...]
    transpose_vectors(0)
    for number, region in enumerate(REGIONS):
        if number == 1:
            for load in small:
                load.wait()
            spread_vectors(atm_vec_ref, vec_ref, 0, tiles)
            spread_vectors(ocn_vec_ref, vec_ref, 1, tiles)
            for place in range(1, 2 * tiles):
                transpose_vectors(place)
        for which, t in region:
            if copies[which][t] is not None:
                copies[which][t].wait()
        for later in REGIONS[max(number + 2, 3) : number + 3]:
            for which, t in later:
                copies[which][t].start()
        for which, t in region:
            total = coefficients(held[which][t], which * tiles + t, level_counts[which])
            if which == 1:
                total = total * sea_ref[t].astype(F32)
            coeff_ref[t, which] = total
    half = tiles // 2
    low, high = coeff_ref[:half], coeff_ref[half:]
    inner_ref[...] = jnp.where(even, high, low)
    outer_ref[...] = jnp.where(even, low, high)


def second_kernel(
    sea_ref,
    atm_class_ref,
    ocn_class_ref,
    inner_ref,
    outer_ref,
    inner_recv_ref,
    outer_recv_ref,
    atm_pair_ref,
    ocn_pair_ref,
    ocn_ref,
    tile_ref,
    next_ref,
    atm_hbm,
    atm_out_hbm,
    ocn_out_hbm,
    atm_ref,
    atm_out_ref,
    ocn_out_ref,
    padded_ref,
    vert_ref,
    column_ref,
    out_sems,
    atm_sems,
):
    tiles, atm_levels, members, columns = atm_hbm.shape
    ocn_levels = ocn_ref.shape[1]
    atm_copies = tile_copies(atm_hbm, each(atm_ref), atm_sems)
    for copy in atm_copies:
        copy.start()
    even = lax.rem(lax.axis_index("tile"), 2) == 0
    quarter = tiles // 2

    @pl.when(even)
    def _():
        for place, ref in enumerate([outer_recv_ref, outer_ref, inner_ref, inner_recv_ref]):
            padded_ref[place * quarter : (place + 1) * quarter] = ref[...]

    @pl.when(jnp.logical_not(even))
    def _():
        for place, ref in enumerate([inner_recv_ref, inner_ref, outer_ref, outer_recv_ref]):
            padded_ref[place * quarter : (place + 1) * quarter] = ref[...]

    group = 16
    sub = lax.broadcasted_iota(jnp.int32, (group, columns), 0)
    row = lax.broadcasted_iota(jnp.int32, (columns, columns), 0)
    col = lax.broadcasted_iota(jnp.int32, (columns, columns), 1)

    def class_weight(number):
        weight = jnp.float32(0.0)
        for value, factor in enumerate(CLASS_TABLE):
            weight = jnp.where(number == value, jnp.float32(factor), weight)
        return weight

    def taper(spread):
        scaled = (row - col).astype(F32) * (1.0 / spread)
        return jnp.exp(-0.5 * scaled * scaled)

    stores = [
        pltpu.make_async_copy(atm_out_ref, atm_out_hbm, out_sems.at[0]),
        pltpu.make_async_copy(ocn_out_ref, ocn_out_hbm, out_sems.at[1]),
    ]
    parts = [
        ([tile_ref, next_ref] + each(atm_ref), atm_out_ref, atm_pair_ref, atm_class_ref, atm_levels, ATM_SPREAD),
        (each(ocn_ref), ocn_out_ref, ocn_pair_ref, ocn_class_ref, ocn_levels, OCN_SPREAD),
    ]

    def weights(which):
        _, _, _, class_ref, _, width = parts[which]
        tapering = taper(width)
        for t in range(tiles):
            spread = jnp.zeros((members, columns), F32)
            for offset in range(2 * HALO + 1):
                spread = spread + class_weight(class_ref[t, offset]) * padded_ref[t + offset, which]
            vert = lax.dot_general(
                tapering, spread, NT, precision=lax.Precision.HIGHEST, preferred_element_type=F32
            ).astype(BF16)
            vert_ref[which, t] = vert
            column_ref[which, t] = vert.astype(F32).T

    def apply(which, t):
        refs, out_ref, pair_ref, _, levels, _ = parts[which]
        ref = refs[t]
        surface = [(levels - KA + i, RISE[i]) for i in range(KA)] if which == 0 else list(enumerate(FALL))
        coupling = dict(surface)
        paired = pair_ref[:, t * columns : (t + 1) * columns]
        for start in range(0, levels, group):
            count = min(group, levels - start)
            plain = [j for j in range(count) if start + j not in coupling]
            total = jnp.zeros((group, columns), F32)
            if plain:
                right = jnp.concatenate([ref[start + j] for j in plain], axis=1)
                product = jnp.dot(
                    vert_ref[which, t, start : start + group, :], right, preferred_element_type=F32
                )
                for place, j in enumerate(plain):
                    part = product[:, place * columns : (place + 1) * columns]
                    total = part if place == 0 else jnp.where(sub == j, part, total)
            for j in range(count):
                level = start + j
                if level in coupling:
                    column = jnp.broadcast_to(
                        column_ref[which, t, :, level : level + 1], (members, columns)
                    )
                    factor = column + paired * (COUPLING * coupling[level])
                    term = jnp.sum(ref[level].astype(F32) * factor, axis=0, keepdims=True)
                    total = jnp.where(sub == j, term, total)
            if which == 1:
                total = total * sea_ref[t].astype(F32)
            out_ref[start : start + count, t, :] = total[:count]

    def finish(which):
        stores[which].start()

    weights(1)
    weights(0)
    for t in range(tiles):
        apply(1, t)
    finish(1)
    apply(0, 0)
    apply(0, 1)
    for t in range(2, tiles):
        atm_copies[t - 2].wait()
        apply(0, t)
    finish(0)
    for store in stores:
        store.wait()


def pair_kernel(
    per_peer,
    pairing_ref,
    recv_ref,
    ocn_hbm,
    atm_hbm,
    atm_pair_ref,
    ocn_pair_ref,
    ocn_ref,
    next_ref,
    sems,
):
    tiles, _, members, columns = ocn_hbm.shape
    copies = tile_copies(ocn_hbm, each(ocn_ref), sems)
    copies.append(pltpu.make_async_copy(atm_hbm.at[1], next_ref, sems.at[tiles]))
    for copy in copies:
        copy.start()
    peers, count = recv_ref.shape[0], recv_ref.shape[1] // 2

    def pair_columns(first, slots):
        rows = recv_ref[:, first : first + count, :].reshape(peers * count, members)
        return lax.dot_general(rows, slots, TN, preferred_element_type=F32)

    atm_pair_ref[...] = pair_columns(count, atm_slots(pairing_ref, columns, tiles, per_peer))
    ocn_pair_ref[...] = pair_columns(0, ocn_slots(columns, tiles, per_peer))
    for copy in copies:
        copy.wait()


def local(atm_anom, ocn_anom, atm_vec, ocn_vec, atm_to_ocean, sea_tiles, atm_class, ocn_class):
    tiles, members, atm_levels, columns = atm_anom.shape
    ocn_levels = ocn_anom.shape[2]
    axes = ("dom", "tile")
    devices = lax.axis_size("dom") * lax.axis_size("tile")
    per_peer = columns // devices
    peer_rows = tiles * per_peer

    by_level = (0, 2, 1, 3)
    atm = jnp.transpose(atm_anom, by_level)
    ocn = jnp.transpose(ocn_anom, by_level)
    atm_rows = jnp.transpose(atm_vec, (1, 0, 2))
    ocn_rows = jnp.transpose(ocn_vec, (1, 0, 2))
    params = pltpu.CompilerParams(vmem_limit_bytes=58 * MIB)

    elements = tiles * members * columns * (atm_levels + ocn_levels)
    top_elements = tiles * members * columns * (KA + KO)
    rest_shape = (tiles - 1,) + atm.shape[1:]
    tops = [
        pltpu.VMEM((tiles - 1, KA, members, columns), BF16),
        pltpu.VMEM((tiles, KO, members, columns), BF16),
        pltpu.SemaphoreType.DMA((2, tiles)),
    ]
    wholes = [pltpu.VMEM(rest_shape, BF16), pltpu.VMEM(ocn.shape, BF16)]
    whole_sems = [pltpu.SemaphoreType.DMA((tiles,)), pltpu.SemaphoreType.DMA((tiles,))]

    def cost(flops, count):
        return pl.CostEstimate(flops=flops, bytes_accessed=2 * count, transcendentals=0)

    outgoing, tile, tile_vec = pl.pallas_call(
        functools.partial(project_kernel, per_peer),
        out_shape=[
            jax.ShapeDtypeStruct((devices, 2 * peer_rows, members), BF16),
            pltpu.VMEM((atm_levels, members, columns), BF16),
            pltpu.VMEM((columns, columns), F32),
        ],
        in_specs=[ANY_SPEC] * 6,
        out_specs=[VMEM_SPEC] * 3,
        scratch_shapes=tops
        + [
            pltpu.SMEM(sea_tiles.shape, jnp.int32),
            pltpu.VMEM(atm_to_ocean.shape, jnp.int32),
            pltpu.VMEM(atm_rows.shape, BF16),
            pltpu.VMEM((KO, tiles, columns), BF16),
            pltpu.SemaphoreType.DMA((5,)),
        ],
        compiler_params=params,
        cost_estimate=cost(4 * top_elements, top_elements),
        name="project",
    )(sea_tiles, atm_to_ocean, atm_rows, ocn_rows, atm, ocn)
    incoming = lax.all_to_all(outgoing, axes, split_axis=0, concat_axis=0, tiled=True)

    edge = pltpu.VMEM((tiles // 2, 2, members, columns), F32)
    inner, outer = pl.pallas_call(
        first_kernel,
        out_shape=[edge, edge],
        in_specs=[ANY_SPEC] * 3 + [VMEM_SPEC] * 2 + [ANY_SPEC] * 2,
        out_specs=[VMEM_SPEC] * 2,
        scratch_shapes=wholes
        + [
            pltpu.SMEM(sea_tiles.shape, jnp.int32),
            pltpu.VMEM(atm_rows.shape, BF16),
            pltpu.VMEM(ocn_rows.shape, BF16),
            pltpu.VMEM((2 * tiles, columns, columns), F32),
            pltpu.VMEM((2 * tiles, 2 * columns, 2 * columns), BF16),
            pltpu.VMEM((tiles, 2, members, columns), F32),
            pltpu.SemaphoreType.DMA((3,)),
        ]
        + whole_sems,
        compiler_params=params,
        cost_estimate=cost(2 * 256 * elements, elements),
        name="first_pass",
    )(sea_tiles, atm_rows, ocn_rows, in_vmem(tile), in_vmem(tile_vec), atm, ocn)

    count = lax.axis_size("tile")
    outer_pairs = [(i, (i + 1) % count if i % 2 else (i - 1) % count) for i in range(count)]
    outer_recv = lax.ppermute(outer, "tile", outer_pairs)
    sent, incoming = lax.optimization_barrier((inner, incoming))
    inner_recv = lax.ppermute(sent, "tile", [(i, i ^ 1) for i in range(count)])

    pair = pltpu.VMEM((members, tiles * columns), F32)
    atm_pair, ocn_pair, ocn_v, next_tile = pl.pallas_call(
        functools.partial(pair_kernel, per_peer),
        out_shape=[
            pair,
            pair,
            pltpu.VMEM(ocn.shape, BF16),
            pltpu.VMEM((atm_levels, members, columns), BF16),
        ],
        in_specs=[VMEM_SPEC, VMEM_SPEC, ANY_SPEC, ANY_SPEC],
        out_specs=[VMEM_SPEC] * 4,
        scratch_shapes=[pltpu.SemaphoreType.DMA((tiles + 1,))],
        compiler_params=pltpu.CompilerParams(vmem_limit_bytes=44 * MIB),
        cost_estimate=cost(40 * top_elements, 4 * top_elements),
        name="pair_columns",
    )(atm_to_ocean, in_vmem(incoming), ocn, atm)

    atm_out, ocn_out = pl.pallas_call(
        second_kernel,
        out_shape=[
            jax.ShapeDtypeStruct((atm_levels, tiles, columns), F32),
            jax.ShapeDtypeStruct((ocn_levels, tiles, columns), F32),
        ],
        in_specs=[SMEM_SPEC] * 3 + [VMEM_SPEC] * 9 + [ANY_SPEC],
        out_specs=[ANY_SPEC] * 2,
        scratch_shapes=[
            pltpu.VMEM((tiles - 2,) + atm.shape[1:], BF16),
            pltpu.VMEM((atm_levels, tiles, columns), F32),
            pltpu.VMEM((ocn_levels, tiles, columns), F32),
            pltpu.VMEM((2 * tiles, 2, members, columns), F32),
            pltpu.VMEM((2, tiles, columns, members), BF16),
            pltpu.VMEM((2, tiles, members, columns), F32),
            pltpu.SemaphoreType.DMA((2,)),
            pltpu.SemaphoreType.DMA((tiles,)),
        ],
        compiler_params=pltpu.CompilerParams(vmem_limit_bytes=42 * MIB),
        cost_estimate=cost(2 * 256 * elements, elements),
        name="second_pass",
    )(
        sea_tiles,
        atm_class,
        ocn_class,
        in_vmem(inner),
        in_vmem(outer),
        in_vmem(inner_recv),
        in_vmem(outer_recv),
        in_vmem(atm_pair),
        in_vmem(ocn_pair),
        in_vmem(ocn_v),
        in_vmem(tile),
        in_vmem(next_tile),
        atm,
    )
    return jnp.transpose(atm_out, (1, 0, 2)), jnp.transpose(ocn_out, (1, 0, 2))


def solution(mesh):
    in_specs = (
        P(("dom", "tile"), None, None, None),
        P(("dom", "tile"), None, None, None),
        P(("dom", "tile"), None, None),
        P(("dom", "tile"), None, None),
        P(("dom", "tile"), None),
        P(("dom", "tile")),
        P(("dom", "tile"), None),
        P(("dom", "tile"), None),
    )
    out_specs = (P(("dom", "tile"), None, None), P(("dom", "tile"), None, None))
    return jax.shard_map(local, mesh=mesh, in_specs=in_specs, out_specs=out_specs, check_vma=False)
```

```python
import functools
import math

import jax
import jax.numpy as jnp
from jax import lax
from jax.experimental import pallas as pl
from jax.experimental.pallas import tpu as pltpu
from jax.sharding import PartitionSpec as P

KA = 16
KO = 16
HALO = 2
GROUP = 4
VECTOR_LEVELS = (31, 19)
REGIONS = [[(0, 0)], [(0, 1)], [(0, 2), (0, 3)], [(1, 0), (1, 1)], [(1, 2), (1, 3)]]

COUPLING = 8.0
ATM_SPREAD = 12.0
OCN_SPREAD = 8.0
CLASS_TABLE = (1.0, 0.7, 0.45, 0.25, 0.0)

BF16 = jnp.bfloat16
F32 = jnp.float32
MIB = 1 << 20
NT = (((1,), (1,)), ((), ()))
TN = (((0,), (0,)), ((), ()))
VMEM_SPEC = pl.BlockSpec(memory_space=pltpu.VMEM)
SMEM_SPEC = pl.BlockSpec(memory_space=pltpu.SMEM)
ANY_SPEC = pl.BlockSpec(memory_space=pl.ANY)

RISE = [math.exp(-2.0 * (KA - 1 - s) / KA) for s in range(KA)]
FALL = [math.exp(-2.0 * o / KO) for o in range(KO)]


def slot_rows(index, columns, tiles, per_peer):
    tile, column = index // columns, index % columns
    return (tile // tiles) * (tiles * per_peer) + (tile % tiles) * per_peer + column % per_peer


def one_hot(rows, width):
    position = lax.broadcasted_iota(jnp.int32, (width, rows.shape[1]), 0)
    return jnp.where(position == rows, 1.0, 0.0).astype(BF16)


def atm_slots(pairing_ref, columns, tiles, per_peer):
    index = jnp.concatenate([pairing_ref[t : t + 1, :] for t in range(tiles)], axis=1)
    return one_hot(slot_rows(index, columns, tiles, per_peer), tiles * columns)


def ocn_slots(columns, tiles, per_peer):
    place = lax.broadcasted_iota(jnp.int32, (1, tiles * columns), 1)
    tile, column = place // columns, place % columns
    rows = (column // per_peer) * (tiles * per_peer) + tile * per_peer + column % per_peer
    return one_hot(rows, tiles * columns)


def in_vmem(array):
    return pltpu.with_memory_space_constraint(array, pltpu.VMEM)


def tile_copies(source, targets, sems):
    first = source.shape[0] - len(targets)
    return [
        pltpu.make_async_copy(source.at[first + i], target, sems.at[i])
        for i, target in enumerate(targets)
    ]


def each(ref):
    return [ref.at[i] for i in range(ref.shape[0])]


def whole_rows(levels):
    return -(-levels // 16) * 16


def spread_vectors(source, levels, vec_ref, which, tiles):
    columns = source.shape[2]
    for t in range(tiles):
        place = which * tiles + t
        vec_ref[place] = jnp.zeros((columns, columns), F32)
        vec_ref[place, :levels] = source[:levels, t, :].astype(F32)


def project_kernel(
    per_peer,
    sea_hbm,
    pairing_hbm,
    atm_vec_hbm,
    ocn_vec_hbm,
    atm_hbm,
    ocn_hbm,
    send_ref,
    tile_ref,
    tile_vec_ref,
    atm_top,
    ocn_top,
    sems,
    sea_ref,
    pairing_ref,
    atm_vec_ref,
    ocn_vec_ref,
    small_sems,
):
    tiles, atm_levels, members, columns = atm_hbm.shape
    start = atm_levels - KA
    peers, count = send_ref.shape[0], send_ref.shape[1] // 2
    small = [
        pltpu.make_async_copy(pairing_hbm, pairing_ref, small_sems.at[0]),
        pltpu.make_async_copy(
            atm_vec_hbm, atm_vec_ref.at[pl.ds(0, atm_levels)], small_sems.at[1]
        ),
        pltpu.make_async_copy(ocn_vec_hbm.at[pl.ds(0, KO)], ocn_vec_ref, small_sems.at[2]),
        pltpu.make_async_copy(sea_hbm, sea_ref, small_sems.at[3]),
    ]
    for load in small:
        load.start()
    atm_tops = [tile_ref.at[pl.ds(start, KA)]] + [atm_top.at[t] for t in range(tiles - 1)]
    loads = [
        [
            pltpu.make_async_copy(atm_hbm.at[t, pl.ds(start, KA)], atm_tops[t], sems.at[0, t]),
            pltpu.make_async_copy(ocn_hbm.at[t, pl.ds(0, KO)], ocn_top.at[t], sems.at[1, t]),
        ]
        for t in range(tiles)
    ]
    for place in range(2):
        for pair in loads:
            pair[place].start()
    rest = pltpu.make_async_copy(
        atm_hbm.at[0, pl.ds(0, start)], tile_ref.at[pl.ds(0, start)], small_sems.at[4]
    )
    rest.start()
    slots = [None, ocn_slots(columns, tiles, per_peer)]
    for load in small:
        load.wait()
    slots[0] = atm_slots(pairing_ref, columns, tiles, per_peer)
    atm_rows = atm_vec_ref[start : start + KA].astype(F32)
    ocn_rows = ocn_vec_ref[...].astype(F32)
    tile_vec_ref[...] = jnp.zeros((columns, columns), F32)
    tile_vec_ref[:atm_levels] = atm_vec_ref[:atm_levels, 0, :].astype(F32)

    def projection(top, t, rows, weights):
        total = jnp.zeros((members, columns), F32)
        for s, weight in enumerate(weights):
            total = total + top[s].astype(F32) * (rows[s, t : t + 1, :] * weight)
        return total

    def route(place, proj):
        rows = lax.dot_general(
            slots[place], jnp.concatenate(proj, axis=1), NT, preferred_element_type=F32
        ).astype(BF16)
        send_ref[:, place * count : (place + 1) * count, :] = rows.reshape(peers, count, members)

    for t in range(tiles):
        loads[t][0].wait()
    atm_proj = [
        projection(atm_tops[t], t, atm_rows, RISE).astype(BF16) for t in range(tiles)
    ]
    for t in range(tiles):
        loads[t][1].wait()
    route(0, atm_proj)
    ocn_proj = [
        (projection(ocn_top.at[t], t, ocn_rows, FALL) * sea_ref[t].astype(F32)).astype(BF16)
        for t in range(tiles)
    ]
    route(1, ocn_proj)
    rest.wait()


def first_kernel(
    sea_hbm,
    atm_vec_hbm,
    ocn_vec_hbm,
    tile_ref,
    tile_vec_ref,
    atm_hbm,
    ocn_hbm,
    inner_ref,
    outer_ref,
    atm_ref,
    ocn_ref,
    sea_ref,
    atm_vec_ref,
    ocn_vec_ref,
    vec_ref,
    weight_ref,
    coeff_ref,
    small_sems,
    atm_sems,
    ocn_sems,
):
    tiles, atm_levels, members, columns = atm_hbm.shape
    ocn_levels = ocn_hbm.shape[1]
    small = [
        pltpu.make_async_copy(
            atm_vec_hbm, atm_vec_ref.at[pl.ds(0, atm_levels)], small_sems.at[0]
        ),
        pltpu.make_async_copy(
            ocn_vec_hbm, ocn_vec_ref.at[pl.ds(0, ocn_levels)], small_sems.at[1]
        ),
        pltpu.make_async_copy(sea_hbm, sea_ref, small_sems.at[2]),
    ]
    for load in small:
        load.start()
    atm_copies = tile_copies(atm_hbm, each(atm_ref), atm_sems)
    ocn_copies = tile_copies(ocn_hbm, each(ocn_ref), ocn_sems)
    copies = [[None] + atm_copies, ocn_copies]
    held = [[tile_ref] + each(atm_ref), each(ocn_ref)]
    for region in REGIONS[1:3]:
        for which, t in region:
            copies[which][t].start()
    even = lax.rem(lax.axis_index("tile"), 2) == 0
    lane = lax.broadcasted_iota(jnp.int32, (members, columns), 1)

    zeros = jnp.zeros((columns, columns), BF16)

    def transpose_vectors(place):
        vec_t = vec_ref[place].T.astype(BF16)
        weight_ref[place, :columns, :columns] = vec_t
        weight_ref[place, :columns, columns:] = zeros
        weight_ref[place, columns:, :columns] = zeros
        weight_ref[place, columns:, columns:] = vec_t

    def coefficients(ref, place, levels):
        vector_levels = VECTOR_LEVELS[place // tiles]
        levels = levels - vector_levels
        half = (levels + 1) // 2
        second = levels - half
        total = jnp.zeros((members, columns), F32)
        for first in range(0, half, GROUP):
            count = min(GROUP, half - first)
            left = ref[first : first + count].reshape(count * members, columns)
            right = ref[second + first : second + first + count].reshape(count * members, columns)
            product = jnp.dot(
                jnp.concatenate([left, right], axis=1),
                weight_ref[place],
                preferred_element_type=F32,
            )
            for j in range(count):
                part = product[j * members : (j + 1) * members]
                total = jnp.where(lane == first + j, part[:, :columns], total)
                total = jnp.where(lane == second + first + j, part[:, columns:], total)
        for level in range(levels, levels + vector_levels):
            product = ref[level].astype(F32) * vec_ref[place, level : level + 1, :]
            total = jnp.where(lane == level, jnp.sum(product, axis=1, keepdims=True), total)
        return total

    level_counts = [atm_levels, ocn_levels]
    vec_ref[0] = tile_vec_ref[...]
    transpose_vectors(0)
    for number, region in enumerate(REGIONS):
        if number == 1:
            for load in small:
                load.wait()
            spread_vectors(atm_vec_ref, atm_levels, vec_ref, 0, tiles)
            spread_vectors(ocn_vec_ref, ocn_levels, vec_ref, 1, tiles)
            for place in range(1, 2 * tiles):
                transpose_vectors(place)
        for which, t in region:
            if copies[which][t] is not None:
                copies[which][t].wait()
        for later in REGIONS[max(number + 2, 3) : number + 3]:
            for which, t in later:
                copies[which][t].start()
        for which, t in region:
            total = coefficients(held[which][t], which * tiles + t, level_counts[which])
            if which == 1:
                total = total * sea_ref[t].astype(F32)
            coeff_ref[t, which] = total
    half = tiles // 2
    low, high = coeff_ref[:half], coeff_ref[half:]
    inner_ref[...] = jnp.where(even, high, low)
    outer_ref[...] = jnp.where(even, low, high)


def second_kernel(
    sea_ref,
    atm_class_ref,
    ocn_class_ref,
    inner_ref,
    outer_ref,
    inner_recv_ref,
    outer_recv_ref,
    atm_pair_ref,
    ocn_pair_ref,
    ocn_ref,
    tile_ref,
    next_ref,
    atm_hbm,
    atm_out_hbm,
    ocn_out_hbm,
    atm_ref,
    atm_out_ref,
    ocn_out_ref,
    padded_ref,
    vert_ref,
    column_ref,
    out_sems,
    atm_sems,
):
    tiles, atm_levels, members, columns = atm_hbm.shape
    ocn_levels = ocn_ref.shape[1]
    atm_copies = tile_copies(atm_hbm, each(atm_ref), atm_sems)
    for copy in atm_copies:
        copy.start()
    even = lax.rem(lax.axis_index("tile"), 2) == 0
    quarter = tiles // 2

    @pl.when(even)
    def _():
        for place, ref in enumerate([outer_recv_ref, outer_ref, inner_ref, inner_recv_ref]):
            padded_ref[place * quarter : (place + 1) * quarter] = ref[...]

    @pl.when(jnp.logical_not(even))
    def _():
        for place, ref in enumerate([inner_recv_ref, inner_ref, outer_ref, outer_recv_ref]):
            padded_ref[place * quarter : (place + 1) * quarter] = ref[...]

    group = 16
    sub = lax.broadcasted_iota(jnp.int32, (group, columns), 0)
    row = lax.broadcasted_iota(jnp.int32, (columns, columns), 0)
    col = lax.broadcasted_iota(jnp.int32, (columns, columns), 1)

    def class_weight(number):
        weight = jnp.float32(0.0)
        for value, factor in enumerate(CLASS_TABLE):
            weight = jnp.where(number == value, jnp.float32(factor), weight)
        return weight

    def taper(spread):
        scaled = (row - col).astype(F32) * (1.0 / spread)
        return jnp.exp(-0.5 * scaled * scaled)

    stores = [
        pltpu.make_async_copy(
            atm_out_ref.at[pl.ds(0, atm_levels)], atm_out_hbm, out_sems.at[0]
        ),
        pltpu.make_async_copy(
            ocn_out_ref.at[pl.ds(0, ocn_levels)], ocn_out_hbm, out_sems.at[1]
        ),
    ]
    parts = [
        ([tile_ref, next_ref] + each(atm_ref), atm_out_ref, atm_pair_ref, atm_class_ref, atm_levels, ATM_SPREAD),
        (each(ocn_ref), ocn_out_ref, ocn_pair_ref, ocn_class_ref, ocn_levels, OCN_SPREAD),
    ]

    def weights(which):
        _, _, _, class_ref, _, width = parts[which]
        tapering = taper(width)
        for t in range(tiles):
            spread = jnp.zeros((members, columns), F32)
            for offset in range(2 * HALO + 1):
                spread = spread + class_weight(class_ref[t, offset]) * padded_ref[t + offset, which]
            vert = lax.dot_general(
                tapering, spread, NT, precision=lax.Precision.HIGHEST, preferred_element_type=F32
            ).astype(BF16)
            vert_ref[which, t] = vert
            column_ref[which, t] = vert.astype(F32).T

    def apply(which, t):
        refs, out_ref, pair_ref, _, levels, _ = parts[which]
        ref = refs[t]
        surface = [(levels - KA + i, RISE[i]) for i in range(KA)] if which == 0 else list(enumerate(FALL))
        coupling = dict(surface)
        paired = pair_ref[:, t * columns : (t + 1) * columns]
        for start in range(0, levels, group):
            count = min(group, levels - start)
            plain = [j for j in range(count) if start + j not in coupling]
            total = jnp.zeros((group, columns), F32)
            if plain:
                right = jnp.concatenate([ref[start + j] for j in plain], axis=1)
                product = jnp.dot(
                    vert_ref[which, t, start : start + group, :], right, preferred_element_type=F32
                )
                for place, j in enumerate(plain):
                    part = product[:, place * columns : (place + 1) * columns]
                    total = part if place == 0 else jnp.where(sub == j, part, total)
            for j in range(count):
                level = start + j
                if level in coupling:
                    column = jnp.broadcast_to(
                        column_ref[which, t, :, level : level + 1], (members, columns)
                    )
                    factor = column + paired * (COUPLING * coupling[level])
                    term = jnp.sum(ref[level].astype(F32) * factor, axis=0, keepdims=True)
                    total = jnp.where(sub == j, term, total)
            if which == 1:
                total = total * sea_ref[t].astype(F32)
            out_ref[start : start + count, t, :] = total[:count]

    def finish(which):
        stores[which].start()

    weights(1)
    weights(0)
    for t in range(tiles):
        apply(1, t)
    finish(1)
    apply(0, 0)
    apply(0, 1)
    for t in range(2, tiles):
        atm_copies[t - 2].wait()
        apply(0, t)
    finish(0)
    for store in stores:
        store.wait()


def pair_kernel(
    per_peer,
    pairing_ref,
    recv_ref,
    ocn_hbm,
    atm_hbm,
    atm_pair_ref,
    ocn_pair_ref,
    ocn_ref,
    next_ref,
    sems,
):
    tiles, _, members, columns = ocn_hbm.shape
    copies = tile_copies(ocn_hbm, each(ocn_ref), sems)
    copies.append(pltpu.make_async_copy(atm_hbm.at[1], next_ref, sems.at[tiles]))
    for copy in copies:
        copy.start()
    peers, count = recv_ref.shape[0], recv_ref.shape[1] // 2

    def pair_columns(first, slots):
        rows = recv_ref[:, first : first + count, :].reshape(peers * count, members)
        return lax.dot_general(rows, slots, TN, preferred_element_type=F32)

    atm_pair_ref[...] = pair_columns(count, atm_slots(pairing_ref, columns, tiles, per_peer))
    ocn_pair_ref[...] = pair_columns(0, ocn_slots(columns, tiles, per_peer))
    for copy in copies:
        copy.wait()


def local(atm_anom, ocn_anom, atm_vec, ocn_vec, atm_to_ocean, sea_tiles, atm_class, ocn_class):
    tiles, members, atm_levels, columns = atm_anom.shape
    ocn_levels = ocn_anom.shape[2]
    axes = ("dom", "tile")
    devices = lax.axis_size("dom") * lax.axis_size("tile")
    per_peer = columns // devices
    peer_rows = tiles * per_peer

    by_level = (0, 2, 1, 3)
    atm = jnp.transpose(atm_anom, by_level)
    ocn = jnp.transpose(ocn_anom, by_level)
    atm_rows = jnp.transpose(atm_vec, (1, 0, 2))
    ocn_rows = jnp.transpose(ocn_vec, (1, 0, 2))
    params = pltpu.CompilerParams(vmem_limit_bytes=58 * MIB)

    elements = tiles * members * columns * (atm_levels + ocn_levels)
    top_elements = tiles * members * columns * (KA + KO)
    rest_shape = (tiles - 1,) + atm.shape[1:]
    tops = [
        pltpu.VMEM((tiles - 1, KA, members, columns), BF16),
        pltpu.VMEM((tiles, KO, members, columns), BF16),
        pltpu.SemaphoreType.DMA((2, tiles)),
    ]
    wholes = [pltpu.VMEM(rest_shape, BF16), pltpu.VMEM(ocn.shape, BF16)]
    whole_sems = [pltpu.SemaphoreType.DMA((tiles,)), pltpu.SemaphoreType.DMA((tiles,))]

    def cost(flops, count):
        return pl.CostEstimate(flops=flops, bytes_accessed=2 * count, transcendentals=0)

    outgoing, tile, tile_vec = pl.pallas_call(
        functools.partial(project_kernel, per_peer),
        out_shape=[
            jax.ShapeDtypeStruct((devices, 2 * peer_rows, members), BF16),
            pltpu.VMEM((atm_levels, members, columns), BF16),
            pltpu.VMEM((columns, columns), F32),
        ],
        in_specs=[ANY_SPEC] * 6,
        out_specs=[VMEM_SPEC] * 3,
        scratch_shapes=tops
        + [
            pltpu.SMEM(sea_tiles.shape, jnp.int32),
            pltpu.VMEM(atm_to_ocean.shape, jnp.int32),
            pltpu.VMEM((whole_rows(atm_levels), tiles, columns), BF16),
            pltpu.VMEM((KO, tiles, columns), BF16),
            pltpu.SemaphoreType.DMA((5,)),
        ],
        compiler_params=params,
        cost_estimate=cost(4 * top_elements, top_elements),
        name="project",
    )(sea_tiles, atm_to_ocean, atm_rows, ocn_rows, atm, ocn)
    incoming = lax.all_to_all(outgoing, axes, split_axis=0, concat_axis=0, tiled=True)

    edge = pltpu.VMEM((tiles // 2, 2, members, columns), F32)
    inner, outer = pl.pallas_call(
        first_kernel,
        out_shape=[edge, edge],
        in_specs=[ANY_SPEC] * 3 + [VMEM_SPEC] * 2 + [ANY_SPEC] * 2,
        out_specs=[VMEM_SPEC] * 2,
        scratch_shapes=wholes
        + [
            pltpu.SMEM(sea_tiles.shape, jnp.int32),
            pltpu.VMEM((whole_rows(atm_levels), tiles, columns), BF16),
            pltpu.VMEM((whole_rows(ocn_levels), tiles, columns), BF16),
            pltpu.VMEM((2 * tiles, columns, columns), F32),
            pltpu.VMEM((2 * tiles, 2 * columns, 2 * columns), BF16),
            pltpu.VMEM((tiles, 2, members, columns), F32),
            pltpu.SemaphoreType.DMA((3,)),
        ]
        + whole_sems,
        compiler_params=params,
        cost_estimate=cost(2 * 256 * elements, elements),
        name="first_pass",
    )(sea_tiles, atm_rows, ocn_rows, in_vmem(tile), in_vmem(tile_vec), atm, ocn)

    count = lax.axis_size("tile")
    outer_pairs = [(i, (i + 1) % count if i % 2 else (i - 1) % count) for i in range(count)]
    outer_recv = lax.ppermute(outer, "tile", outer_pairs)
    sent, incoming = lax.optimization_barrier((inner, incoming))
    inner_recv = lax.ppermute(sent, "tile", [(i, i ^ 1) for i in range(count)])

    pair = pltpu.VMEM((members, tiles * columns), F32)
    atm_pair, ocn_pair, ocn_v, next_tile = pl.pallas_call(
        functools.partial(pair_kernel, per_peer),
        out_shape=[
            pair,
            pair,
            pltpu.VMEM(ocn.shape, BF16),
            pltpu.VMEM((atm_levels, members, columns), BF16),
        ],
        in_specs=[VMEM_SPEC, VMEM_SPEC, ANY_SPEC, ANY_SPEC],
        out_specs=[VMEM_SPEC] * 4,
        scratch_shapes=[pltpu.SemaphoreType.DMA((tiles + 1,))],
        compiler_params=pltpu.CompilerParams(vmem_limit_bytes=44 * MIB),
        cost_estimate=cost(40 * top_elements, 4 * top_elements),
        name="pair_columns",
    )(atm_to_ocean, in_vmem(incoming), ocn, atm)

    atm_out, ocn_out = pl.pallas_call(
        second_kernel,
        out_shape=[
            jax.ShapeDtypeStruct((atm_levels, tiles, columns), F32),
            jax.ShapeDtypeStruct((ocn_levels, tiles, columns), F32),
        ],
        in_specs=[SMEM_SPEC] * 3 + [VMEM_SPEC] * 9 + [ANY_SPEC],
        out_specs=[ANY_SPEC] * 2,
        scratch_shapes=[
            pltpu.VMEM((tiles - 2,) + atm.shape[1:], BF16),
            pltpu.VMEM((whole_rows(atm_levels), tiles, columns), F32),
            pltpu.VMEM((whole_rows(ocn_levels), tiles, columns), F32),
            pltpu.VMEM((2 * tiles, 2, members, columns), F32),
            pltpu.VMEM((2, tiles, columns, members), BF16),
            pltpu.VMEM((2, tiles, members, columns), F32),
            pltpu.SemaphoreType.DMA((2,)),
            pltpu.SemaphoreType.DMA((tiles,)),
        ],
        compiler_params=pltpu.CompilerParams(vmem_limit_bytes=42 * MIB),
        cost_estimate=cost(2 * 256 * elements, elements),
        name="second_pass",
    )(
        sea_tiles,
        atm_class,
        ocn_class,
        in_vmem(inner),
        in_vmem(outer),
        in_vmem(inner_recv),
        in_vmem(outer_recv),
        in_vmem(atm_pair),
        in_vmem(ocn_pair),
        in_vmem(ocn_v),
        in_vmem(tile),
        in_vmem(next_tile),
        atm,
    )
    return jnp.transpose(atm_out, (1, 0, 2)), jnp.transpose(ocn_out, (1, 0, 2))


def solution(mesh):
    in_specs = (
        P(("dom", "tile"), None, None, None),
        P(("dom", "tile"), None, None, None),
        P(("dom", "tile"), None, None),
        P(("dom", "tile"), None, None),
        P(("dom", "tile"), None),
        P(("dom", "tile")),
        P(("dom", "tile"), None),
        P(("dom", "tile"), None),
    )
    out_specs = (P(("dom", "tile"), None, None), P(("dom", "tile"), None, None))
    return jax.shard_map(local, mesh=mesh, in_specs=in_specs, out_specs=out_specs, check_vma=False)
```
